32 devices in a mesh: grp: 8 (over z, core), dev: 4 (over y, x).
Axes of the slice: x: 2, y: 2, z: 4, core: 2. Of those that a mesh axis runs over, the one named last changes fastest.
Arguments:
- residual: bfloat16 [128, 7168], P(('grp', 'dev')), may hold values from -6 to 6
- routes: int32 [128, 2], P(('grp', 'dev')), may hold values from 0 to 3, all different within a row; in each aligned block of 4 rows (0 to 3, 4 to 7, ...) at most 3 rows name the same one
- gate_weights: bfloat16 [128, 2], P(('grp', 'dev')), may hold values from 0.19921875 to 1.5
- moe_gain: bfloat16 [7168], replicated, may hold values from 0.25 to 1.75
- attn_gain: bfloat16 [7168], replicated, may hold values from 0.25 to 1.75
- kv_gain: bfloat16 [512], replicated, may hold values from 0.25 to 1.75
- w_gate: bfloat16 [7168, 4096], P(None, 'dev'), may hold values from -0.0625 to 0.0625
- w_up: bfloat16 [7168, 4096], P(None, 'dev'), may hold values from -0.0625 to 0.0625
- w_down: bfloat16 [4096, 7168], P('dev'), may hold values from -0.1875 to 0.1875
- w_kv: bfloat16 [7168, 576], P('grp'), may hold values from -0.0625 to 0.0625
- q_lat: bfloat16 [128, 64, 512], P(('grp', 'dev')), may hold values from -24 to 24
- q_rope: bfloat16 [128, 64, 64], P(('grp', 'dev')), may hold values from -24 to 24
- cache_lat: bfloat16 [384, 128, 512], P(('grp', 'dev')), may hold values from -12 to 12
- cache_rope: bfloat16 [384, 64, 128], P(('grp', 'dev')), may hold values from -12 to 12
- page_table: int32 [128, 4], P(('grp', 'dev')), may hold values from 0 to 11, as said below
- lengths: int32 [128], P(('grp', 'dev')), may hold values from 1 to 511
Outputs:
- residual_next: bfloat16 [128, 7168], P(('grp', 'dev'))
- new_entry: bfloat16 [128, 576], P(('grp', 'dev'))
- attn_out: bfloat16 [128, 64, 512], P(('grp', 'dev'))
The draws below stay inside these ranges and needn't reach their ends.
Inputs may be any that keep to these rules, and one draw needn't show every extreme that they name: In the 4 rows of one device no expert is named by more than 3 routes. `page_table`: entries are pages of the pool of the request's own device; the requests of one device share their first page.
All inputs are finite; a program needn't handle non-finite values.
Results may differ from the reference program's by a relative error of at most 0.0068.
Values may be sent and summed in bfloat16 or wider, within the bound.
A program may use at most 128 MiB of HBM per device.

```python
import math
import jax
import jax.numpy as jnp
import numpy as np
from jax import lax

D = 7168
HEADS = 64
LAT = 512
ROPE = 64
FE = 1024
EXPERTS = 4
TOP = 2
PAGE = 128
PAGES_REQ = 4
POOL_DEV = 12
TOK_DEV = 4
CAP = 3
SHARDS = 1
UNITS = 1024
TOKENS = 128
POOL = 384


def draw_q_lat(key, part):
    key = jax.random.fold_in(key, 1)
    values = jax.random.normal(key, (TOKENS, HEADS, LAT), jnp.float32)
    return values.astype(jnp.bfloat16)


def draw_q_rope(key, part):
    key = jax.random.fold_in(key, 2)
    values = jax.random.normal(key, (TOKENS, HEADS, ROPE), jnp.float32)
    return values.astype(jnp.bfloat16)


def draw_cache_lat(key, part):
    key = jax.random.fold_in(key, 3)
    values = jax.random.normal(key, (POOL, PAGE, LAT), jnp.float32)
    return values.astype(jnp.bfloat16)


def draw_cache_rope(key, part):
    key = jax.random.fold_in(key, 4)
    values = jax.random.normal(key, (POOL, ROPE, PAGE), jnp.float32)
    return values.astype(jnp.bfloat16)


def draw_page_table(key, part):
    key = jax.random.fold_in(key, 5)
    blocks = TOKENS // TOK_DEV
    shared = jax.random.randint(jax.random.fold_in(key, 1), (blocks, 1, 1), 0, POOL_DEV)
    others = jax.random.randint(jax.random.fold_in(key, 2), (blocks, TOK_DEV, PAGES_REQ), 0, POOL_DEV)
    table = jnp.where(jnp.arange(PAGES_REQ)[None, None, :] == 0, shared, others).reshape(TOKENS, PAGES_REQ)
    table = table.at[0, 1].set(POOL_DEV - 1).at[0, 2].set(0)
    return table.astype(jnp.int32)


def draw_lengths(key, part):
    key = jax.random.fold_in(key, 6)
    values = jax.random.randint(key, (TOKENS,), 1, PAGES_REQ * PAGE)
    values = values.at[0].set(PAGES_REQ * PAGE - 1).at[1].set(1)
    return values.astype(jnp.int32)


def level_of(rng, dims, cuts, least, top_value):
    loudness = 1.0
    for axis_at, blocks in cuts:
        heights = jax.random.uniform(jax.random.fold_in(jax.random.fold_in(rng, 6), axis_at), (blocks,), jnp.float32, least / len(cuts), top_value / len(cuts))
        loudness = loudness * jnp.repeat(jnp.exp(heights), dims[axis_at] // blocks).reshape((-1,) + (1,) * (len(dims) - 1 - axis_at))
    return loudness


def shared_out(key, own, number, rows, number_of, top, most, slope):
    order = jax.random.permutation(key, number_of)
    crowded, ordinary = portions_of(number_of, rows * top, most, slope, True), portions_of(number_of, rows * top, most, slope, False)
    places = jnp.arange(number_of)

    def named(sizes, offset_by):
        used = int((sizes > 0).sum())
        fixed = max(1, used // 4)
        moved = fixed + (places - fixed + offset_by * (used - fixed)) % max(1, number_of - fixed)
        return jnp.zeros((number_of,), jnp.int32).at[order[jnp.where(places < fixed, places, moved)]].set(jnp.asarray(sizes, jnp.int32))

    sizes = jnp.where(number % 4 == 0, named(crowded, number // 4), named(ordinary, number - number // 4 - 1))
    mixed = jax.random.permutation(jax.random.fold_in(own, 3), number_of)
    donor, taker = mixed[0:number_of // 2 * 2:2], mixed[1:number_of // 2 * 2:2]
    room = jnp.minimum(sizes[donor] - 1, most - sizes[taker]) // 2
    room = jnp.where((donor == order[0]) | (taker == order[0]) | (sizes[taker] == 0), 0, jnp.maximum(room, 0))
    moved = jax.random.randint(jax.random.fold_in(own, 4), (number_of // 2,), 0, 1 << 20) % (room + 1)
    sizes = sizes.at[donor].add(-moved).at[taker].add(moved)
    items = jnp.searchsorted(jnp.cumsum(sizes), jnp.arange(rows * top), side="right").astype(jnp.int32)
    grid = items.reshape(top, rows).T
    grid = grid[jax.random.permutation(jax.random.fold_in(own, 1), rows)]
    offset_by = jax.random.randint(jax.random.fold_in(own, 2), (rows, 1), 0, top)
    return jnp.take_along_axis(grid, (jnp.arange(top)[None, :] + offset_by) % top, axis=1)


def portions_of(amount, total, most, skew, full):
    loads = [(1 << 20) // math.isqrt(standing ** skew) + 1 for standing in range(1, amount + 1)]
    largest = most if full else min(most, max(-(-total // amount), total * loads[0] // sum(loads)))
    least = 1 if total - largest >= amount - 1 else 0
    given, rest = [largest] + [least] * (amount - 1), total - largest - least * (amount - 1)
    while rest > 0:
        movable = [i for i in range(1, amount) if given[i] < largest] or [i for i in range(1, amount) if given[i] < most]
        whole, remaining = sum([loads[i] for i in movable]), rest
        for i in movable:
            more = min(most - given[i], max(1, remaining * loads[i] // whole), rest)
            given[i] = given[i] + more
            rest = rest - more
    return np.array(given)


def scatter_about(key, extent, deviation, bound, cuts=(), held_as=jnp.bfloat16):
    result = deviation * jax.random.normal(key, extent, jnp.float32)
    if cuts:
        result = result * level_of(key, extent, cuts, -0.22, 0.18)
    return jnp.clip(result, -bound, bound).astype(held_as)


def setup_inputs(seed: int = 0) -> dict:
    keys = jax.random.split(jax.random.key(seed), 17)
    residual = scatter_about(keys[0], (TOKENS, D), 1.0, 6.0, ((0, 32),))
    routes_keys = jax.random.split(jax.random.fold_in(keys[1], 1), TOKENS // TOK_DEV)
    routes_turns = jax.random.permutation(jax.random.fold_in(keys[1], 3), TOKENS // TOK_DEV)
    routes = jax.vmap(lambda own, number: shared_out(jax.random.fold_in(keys[1], 2), own, number, TOK_DEV, EXPERTS, TOP, CAP, 2))(routes_keys, routes_turns).reshape((TOKENS, TOP))
    gate_weights = jnp.clip(0.19921875 + 1.3007812 * jax.random.uniform(keys[2], (TOKENS, TOP), jnp.float32) ** level_of(keys[2], (TOKENS, TOP), ((0, 32),), -0.2, 0.2), 0.19921875, 1.5).astype(jnp.bfloat16)
    moe_gain = jnp.clip(1.0 + 0.15 * jax.random.normal(keys[3], (D,), jnp.float32), 0.25, 1.75).astype(jnp.bfloat16)
    attn_gain = jnp.clip(1.0 + 0.15 * jax.random.normal(keys[4], (D,), jnp.float32), 0.25, 1.75).astype(jnp.bfloat16)
    kv_gain = jnp.clip(1.0 + 0.15 * jax.random.normal(keys[5], (LAT,), jnp.float32), 0.25, 1.75).astype(jnp.bfloat16)
    w_gate = scatter_about(keys[6], (D, EXPERTS * FE), D ** -0.5, 0.0625, ((1, 4),))
    w_up = scatter_about(keys[7], (D, EXPERTS * FE), D ** -0.5, 0.0625, ((1, 4),))
    w_down = scatter_about(keys[8], (EXPERTS * FE, D), FE ** -0.5, 0.1875, ((0, 4),))
    w_kv = scatter_about(keys[9], (D, LAT + ROPE), D ** -0.5, 0.0625, ((0, 8),))
    q_lat = draw_q_lat(jax.random.fold_in(keys[16], 71), 0)
    q_rope = draw_q_rope(jax.random.fold_in(keys[16], 71), 0)
    cache_lat = draw_cache_lat(jax.random.fold_in(keys[16], 71), 0)
    cache_rope = draw_cache_rope(jax.random.fold_in(keys[16], 71), 0)
    page_table = draw_page_table(jax.random.fold_in(keys[16], 71), 0)
    lengths = draw_lengths(jax.random.fold_in(keys[16], 71), 0)
    return dict(residual=residual, routes=routes, gate_weights=gate_weights, moe_gain=moe_gain, attn_gain=attn_gain, kv_gain=kv_gain, w_gate=w_gate, w_up=w_up, w_down=w_down, w_kv=w_kv, q_lat=q_lat, q_rope=q_rope, cache_lat=cache_lat, cache_rope=cache_rope, page_table=page_table, lengths=lengths)


epsilon = 1e-06
score_scale = 192.0 ** (-0.5)

def rms_scale(values, gain):
    widened = values.astype(jnp.float32)
    return widened * lax.rsqrt(lax.optimization_barrier(jnp.mean(widened * widened, axis=-1, keepdims=True)) + epsilon) * gain.astype(jnp.float32)

def new_key(kv_rows, kv_gain, lengths):
    latent = rms_scale(kv_rows[:, :LAT], kv_gain)
    half_width = ROPE // 2
    freqs = 10000.0 ** (-(2.0 * jnp.arange(half_width, dtype=jnp.float32)) / ROPE)
    angle = lengths.astype(jnp.float32)[:, None] * freqs[None, :]
    first_half = kv_rows[:, LAT:LAT + half_width]
    second_half = kv_rows[:, LAT + half_width:]
    rotated = jnp.concatenate([first_half * jnp.cos(angle) - second_half * jnp.sin(angle), second_half * jnp.cos(angle) + first_half * jnp.sin(angle)], axis=1)
    return jnp.concatenate([latent, rotated], axis=1).astype(jnp.bfloat16)

def attend(pieces):
    q_lat, q_rope, cache_lat, cache_rope, page_table, lengths, new_entry = pieces
    token_count = q_lat.shape[0]
    key_span = PAGES_REQ * PAGE
    highest = lax.Precision.HIGHEST
    keys_lat = cache_lat[page_table].reshape(token_count, key_span, LAT).astype(jnp.float32)
    keys_rope = cache_rope[page_table].astype(jnp.float32)
    query_lat = q_lat.astype(jnp.float32)
    query_rope = q_rope.astype(jnp.float32)
    score_lat = jnp.einsum('thc,tlc->thl', query_lat, keys_lat, precision=highest)
    score_rope = jnp.einsum('thr,tpru->thpu', query_rope, keys_rope, precision=highest).reshape(token_count, HEADS, key_span)
    scores = (score_lat + score_rope) * score_scale
    new_lat = new_entry[:, :LAT].astype(jnp.float32)
    new_rope = new_entry[:, LAT:].astype(jnp.float32)
    self_score = (jnp.einsum('thc,tc->th', query_lat, new_lat, precision=highest) + jnp.einsum('thr,tr->th', query_rope, new_rope, precision=highest)) * score_scale
    live_mask = (jnp.arange(key_span, dtype=jnp.int32)[None, :] < lengths[:, None])[:, None, :]
    masked = jnp.where(live_mask, scores, -1e+30)
    largest = jnp.maximum(lax.optimization_barrier(jnp.max(masked, axis=2)), self_score)
    exps = jnp.where(live_mask, jnp.exp(masked - largest[:, :, None]), 0.0)
    self_exp = jnp.exp(self_score - largest)
    total = lax.optimization_barrier(jnp.sum(exps, axis=2)) + self_exp
    probs = lax.optimization_barrier(exps.astype(jnp.bfloat16)).astype(jnp.float32)
    self_prob = lax.optimization_barrier(self_exp.astype(jnp.bfloat16)).astype(jnp.float32)
    summed = jnp.einsum('thl,tlc->thc', probs, keys_lat, precision=highest) + self_prob[:, :, None] * new_lat[:, None, :]
    return (summed / total[:, :, None]).astype(jnp.bfloat16)

def reference(residual, routes, gate_weights, moe_gain, attn_gain, kv_gain, w_gate, w_up, w_down, w_kv, q_lat, q_rope, cache_lat, cache_rope, page_table, lengths):
    moe_in = rms_scale(residual, moe_gain).astype(jnp.bfloat16)
    blocks = TOKENS // TOK_DEV
    route_count = TOK_DEV * TOP
    flat_routes = routes.reshape(blocks, route_count)
    expert_ids = jnp.arange(EXPERTS, dtype=jnp.int32)
    onehot = (flat_routes[:, :, None] == expert_ids[None, None, :]).astype(jnp.int32)
    slot_index = lax.optimization_barrier(jnp.sum((jnp.cumsum(onehot, axis=1) - onehot) * onehot, axis=2))
    picked = ((flat_routes[:, None, None, :] == expert_ids[None, :, None, None]) & (slot_index[:, None, None, :] == jnp.arange(CAP, dtype=jnp.int32)[None, None, :, None])).astype(jnp.int32)
    route_token = jnp.arange(route_count, dtype=jnp.int32) // TOP
    local_token = lax.optimization_barrier(jnp.sum(picked * route_token[None, None, None, :], axis=3))
    token_index = local_token + (jnp.arange(blocks, dtype=jnp.int32) * TOK_DEV)[:, None, None]
    slot_weight = lax.optimization_barrier(jnp.sum(picked.astype(jnp.float32) * gate_weights.reshape(blocks, route_count).astype(jnp.float32)[:, None, None, :], axis=3))
    moe_out = jnp.zeros((TOKENS, D), jnp.float32)
    for expert in range(EXPERTS):
        rows_index = token_index[:, expert, :].reshape(-1).astype(jnp.int32)
        route_weight = slot_weight[:, expert, :].reshape(-1)
        picked_rows = moe_in[rows_index]
        gate_proj = jnp.dot(picked_rows, w_gate[:, expert * FE:(expert + 1) * FE], preferred_element_type=jnp.float32)
        up_proj = jnp.dot(picked_rows, w_up[:, expert * FE:(expert + 1) * FE], preferred_element_type=jnp.float32)
        hidden = (jax.nn.silu(gate_proj) * up_proj).astype(jnp.bfloat16)
        hidden_parts = hidden.reshape(-1, SHARDS, UNITS).transpose(1, 0, 2)
        down_parts = w_down[expert * FE:(expert + 1) * FE].reshape(SHARDS, UNITS, D)

        def add_shard(running, shard_pair):
            shard_part = jnp.dot(shard_pair[0], shard_pair[1], preferred_element_type=jnp.float32).astype(jnp.bfloat16)
            return (running + shard_part.astype(jnp.float32), None)
        summed, _ = lax.scan(add_shard, jnp.zeros((rows_index.shape[0], D), jnp.float32), (hidden_parts, down_parts))
        moe_out = moe_out.at[rows_index].add(route_weight[:, None] * summed)
    residual_next = (residual.astype(jnp.float32) + moe_out).astype(jnp.bfloat16)
    attn_in = rms_scale(residual_next, attn_gain).astype(jnp.bfloat16)
    kv_rows = jnp.dot(attn_in, w_kv, preferred_element_type=jnp.float32)
    new_entry = new_key(kv_rows, kv_gain, lengths)
    attn_out = lax.map(attend, (q_lat.reshape(blocks, TOK_DEV, HEADS, LAT), q_rope.reshape(blocks, TOK_DEV, HEADS, ROPE), cache_lat.reshape(blocks, POOL_DEV, PAGE, LAT), cache_rope.reshape(blocks, POOL_DEV, ROPE, PAGE), page_table.reshape(blocks, TOK_DEV, PAGES_REQ), lengths.reshape(blocks, TOK_DEV), new_entry.reshape(blocks, TOK_DEV, LAT + ROPE)))
    return (residual_next, new_entry, attn_out.reshape(TOKENS, HEADS, LAT))
```

```python
import functools
import math

import jax
import jax.numpy as jnp
from jax import lax
from jax.experimental import pallas as pl
from jax.experimental.pallas import tpu as pltpu
from jax.sharding import PartitionSpec as P

WIDTH = 7168
HEADS = 64
LAT = 512
ROPE = 64
EXPERTS = 4
TOP = 2
PAGE = 128
PAGES_REQ = 4
CAP = 3


epsilon = 1e-06
score_scale = 192.0 ** (-0.5)


def rms_scale(values, gain):
    widened = values.astype(jnp.float32)
    return (
        widened
        * lax.rsqrt(jnp.mean(widened * widened, axis=-1, keepdims=True) + epsilon)
        * gain.astype(jnp.float32)
    )


def expert_part(picked_rows, w_gate, w_up, w_down):
    gate_proj = jnp.dot(picked_rows, w_gate, preferred_element_type=jnp.float32)
    up_proj = jnp.dot(picked_rows, w_up, preferred_element_type=jnp.float32)
    hidden = (jax.nn.silu(gate_proj) * up_proj).astype(jnp.bfloat16)
    return jnp.dot(hidden, w_down, preferred_element_type=jnp.float32).astype(jnp.bfloat16)


def new_key(kv_rows, kv_gain, lengths):
    latent = rms_scale(kv_rows[:, :LAT], kv_gain)
    half_width = ROPE // 2
    freqs = 10000.0 ** (-(2.0 * jnp.arange(half_width, dtype=jnp.float32)) / ROPE)
    angle = lengths.astype(jnp.float32)[:, None] * freqs[None, :]
    first_half = kv_rows[:, LAT : LAT + half_width]
    second_half = kv_rows[:, LAT + half_width :]
    rotated = jnp.concatenate(
        [
            first_half * jnp.cos(angle) - second_half * jnp.sin(angle),
            second_half * jnp.cos(angle) + first_half * jnp.sin(angle),
        ],
        axis=1,
    )
    return jnp.concatenate([latent, rotated], axis=1).astype(jnp.bfloat16)


def attend(q_lat, q_rope, cache_lat, cache_rope, page_table, lengths, new_entry):
    token_count = q_lat.shape[0]
    key_span = PAGES_REQ * PAGE
    keys_lat = cache_lat[page_table].reshape(token_count, key_span, LAT)
    keys_rope = cache_rope[page_table]
    score_lat = jnp.einsum("thc,tlc->thl", q_lat, keys_lat, preferred_element_type=jnp.float32)
    score_rope = jnp.einsum(
        "thr,tpru->thpu", q_rope, keys_rope, preferred_element_type=jnp.float32
    ).reshape(token_count, HEADS, key_span)
    scores = (score_lat + score_rope) * score_scale
    new_lat = new_entry[:, :LAT]
    new_rope = new_entry[:, LAT:]
    self_score = (
        jnp.einsum("thc,tc->th", q_lat, new_lat, preferred_element_type=jnp.float32)
        + jnp.einsum("thr,tr->th", q_rope, new_rope, preferred_element_type=jnp.float32)
    ) * score_scale
    live_mask = (jnp.arange(key_span, dtype=jnp.int32)[None, :] < lengths[:, None])[:, None, :]
    masked = jnp.where(live_mask, scores, -1e30)
    largest = jnp.maximum(jnp.max(masked, axis=2), self_score)
    exps = jnp.where(live_mask, jnp.exp(masked - largest[:, :, None]), 0.0)
    self_exp = jnp.exp(self_score - largest)
    total = jnp.sum(exps, axis=2) + self_exp
    summed = jnp.einsum(
        "thl,tlc->thc", exps.astype(jnp.bfloat16), keys_lat, preferred_element_type=jnp.float32
    )
    self_prob = lax.optimization_barrier(self_exp.astype(jnp.bfloat16)).astype(jnp.float32)
    summed = summed + self_prob[:, :, None] * new_lat.astype(jnp.float32)[:, None, :]
    return (summed / total[:, :, None]).astype(jnp.bfloat16)


def local(
    residual,
    routes,
    gate_weights,
    moe_gain,
    attn_gain,
    kv_gain,
    w_gate,
    w_up,
    w_down,
    w_kv,
    q_lat,
    q_rope,
    cache_lat,
    cache_rope,
    page_table,
    lengths,
):
    token_count = residual.shape[0]
    moe_in = rms_scale(residual, moe_gain).astype(jnp.bfloat16)
    group_size = lax.axis_size("dev")
    shards = group_size // EXPERTS
    expert_ids = jnp.arange(EXPERTS, dtype=jnp.int32)
    flat_routes = routes.reshape(-1)
    onehot = (flat_routes[:, None] == expert_ids[None, :]).astype(jnp.int32)
    slot_index = jnp.sum((jnp.cumsum(onehot, axis=0) - onehot) * onehot, axis=1)
    picked = (
        (flat_routes[None, None, :] == expert_ids[:, None, None])
        & (slot_index[None, None, :] == jnp.arange(CAP, dtype=jnp.int32)[None, :, None])
    ).astype(jnp.float32)
    picked = picked.reshape(EXPERTS, CAP, token_count, TOP)
    placing = jnp.sum(picked, axis=3).astype(jnp.bfloat16)
    per_expert = jnp.einsum(
        "ect,td->ecd", placing, moe_in, preferred_element_type=jnp.float32
    ).astype(jnp.bfloat16)
    outgoing = jnp.repeat(per_expert, shards, axis=0)
    arrived = lax.all_to_all(outgoing, "dev", split_axis=0, concat_axis=0, tiled=True)
    sources, slot_count, feature_width = arrived.shape
    expert_rows = expert_part(
        arrived.reshape(sources * slot_count, feature_width), w_gate, w_up, w_down
    )
    returned = lax.all_to_all(
        expert_rows.reshape(sources, slot_count, feature_width),
        "dev",
        split_axis=0,
        concat_axis=0,
        tiled=True,
    )
    shard_sums = jnp.sum(returned.astype(jnp.float32).reshape(EXPERTS, shards, CAP, -1), axis=1)
    combine = jnp.einsum(
        "ectk,tk->tec", picked, gate_weights.astype(jnp.float32), precision=lax.Precision.HIGHEST
    )
    moe_out = jnp.einsum("tec,ecd->td", combine, shard_sums, precision=lax.Precision.HIGHEST)
    residual_next = (residual.astype(jnp.float32) + moe_out).astype(jnp.bfloat16)
    attn_in = rms_scale(residual_next, attn_gain).astype(jnp.bfloat16)
    column_rows = lax.all_to_all(attn_in, "grp", split_axis=1, concat_axis=0, tiled=True)
    kv_rows = lax.psum_scatter(
        jnp.dot(column_rows, w_kv, preferred_element_type=jnp.float32),
        "grp",
        scatter_dimension=0,
        tiled=True,
    )
    new_entry = new_key(kv_rows, kv_gain, lengths)
    attn_out = attend(q_lat, q_rope, cache_lat, cache_rope, page_table, lengths, new_entry)
    return (residual_next, new_entry, attn_out)


def fused_kernel(
    group_count,
    dev_count,
    residual_ref,
    routes_ref,
    gates_ref,
    moe_gain_ref,
    attn_gain_ref,
    kv_gain_ref,
    lengths_ref,
    lengths_smem,
    table_smem,
    w_gate_hbm,
    w_up_hbm,
    w_down_hbm,
    w_kv_hbm,
    q_lat_hbm,
    q_rope_hbm,
    cache_lat_hbm,
    cache_rope_hbm,
    out_residual,
    out_entry,
    out_attn,
    w_gate,
    w_up,
    w_down,
    w_kv,
    q_lat,
    q_rope,
    cache_lat,
    cache_rope,
    pack32,
    disp_send,
    disp_recv,
    rows32,
    rows16,
    gate_acc,
    up_acc,
    hidden,
    combine,
    residual_pack,
    gain_pack,
    next_pack,
    square_acc,
    ret_send,
    ret_recv,
    col_send,
    col_recv,
    col32,
    part_send,
    part_recv,
    attn_acc,
    attn_max,
    attn_sum,
    rope_cos,
    rope_sin,
    next32,
    load_sem,
    gate_sem,
    up_sem,
    down_sem,
    disp_send_sem,
    disp_recv_sem,
    ret_send_sem,
    ret_recv_sem,
    col_send_sem,
    col_recv_sem,
    part_send_sem,
    part_recv_sem,
):
    f32 = jnp.float32
    bf16 = jnp.bfloat16
    me_g = lax.axis_index("grp")
    me_d = lax.axis_index("dev")
    tokens, width = residual_ref.shape
    quarter = width // 4
    chunks = group_count // 2
    block = width // group_count
    k_chunks, k_rows, _ = w_gate.shape
    down_cols = width // chunks
    pack_width = col_send.shape[-1]
    widths = [min(pack_width, block - q * pack_width) for q in range(4)]

    def remote(src, dst, send, recv, grp, dev):
        return pltpu.make_async_remote_copy(
            src_ref=src,
            dst_ref=dst,
            send_sem=send,
            recv_sem=recv,
            device_id=(grp, dev),
            device_id_type=pl.DeviceIdType.MESH,
        )

    barrier = pltpu.get_barrier_semaphore()
    for r in range(1, dev_count):
        pl.semaphore_signal(
            barrier,
            inc=1,
            device_id=(me_g, lax.rem(me_d + r, dev_count)),
            device_id_type=pl.DeviceIdType.MESH,
        )
    for r in range(1, group_count):
        pl.semaphore_signal(
            barrier,
            inc=1,
            device_id=(lax.rem(me_g + r, group_count), me_d),
            device_id_type=pl.DeviceIdType.MESH,
        )

    loads = [
        pltpu.make_async_copy(src, dst, load_sem.at[at])
        for at, (src, dst) in enumerate(
            [
                (q_lat_hbm, q_lat),
                (q_rope_hbm, q_rope),
                (cache_lat_hbm, cache_lat),
                (cache_rope_hbm, cache_rope),
                (w_kv_hbm, w_kv),
            ]
        )
    ]
    for load in loads[:4]:
        load.start()

    def gate_copy(k):
        return pltpu.make_async_copy(
            w_gate_hbm.at[pl.ds(k * k_rows, k_rows), :], w_gate.at[k], gate_sem.at[k]
        )

    def up_copy(k):
        return pltpu.make_async_copy(
            w_up_hbm.at[pl.ds(k * k_rows, k_rows), :], w_up.at[k], up_sem.at[k]
        )

    def chunk_at(step):
        return lax.rem(me_g // 2 + 1 + step, chunks)

    def down_copy(step):
        start = pl.multiple_of(chunk_at(step) * down_cols, 128)
        return pltpu.make_async_copy(
            w_down_hbm.at[:, pl.ds(start, down_cols)], w_down.at[step], down_sem.at[step]
        )

    for k in range(k_chunks):
        gate_copy(k).start()
        up_copy(k).start()
    for step in range(chunks):
        down_copy(step).start()
    loads[4].start()

    residual = residual_ref[...].astype(f32)
    moe_in = (
        residual
        * lax.rsqrt(jnp.mean(residual * residual, axis=1, keepdims=True) + epsilon)
        * moe_gain_ref[...].astype(f32)
    )
    for q in range(4):
        pack32[tokens * q : tokens * (q + 1), :] = moe_in[:, q * quarter : (q + 1) * quarter]
    packed = pack32[...].astype(bf16)
    disp_send[...] = packed
    disp_recv[me_d] = packed

    pl.semaphore_wait(barrier, dev_count - 1 + group_count - 1)

    def disp_copy(r):
        dest = lax.rem(me_d + r, dev_count)
        return remote(
            disp_send, disp_recv.at[me_d], disp_send_sem.at[r], disp_recv_sem.at[me_d], me_g, dest
        )

    for r in range(1, dev_count):
        disp_copy(r).start()

    routes = routes_ref[...]
    gates = gates_ref[...].astype(f32)
    for e in range(dev_count):
        weight = jnp.sum(jnp.where(routes == e, gates, 0.0), axis=1, keepdims=True)
        weight = jnp.broadcast_to(weight, (tokens, 128))
        for q in range(4):
            combine[e, tokens * q : tokens * (q + 1), :] = weight
    residual_pack[...] = jnp.zeros_like(residual_pack)
    gain_pack[...] = jnp.zeros_like(gain_pack)
    attn_gain = attn_gain_ref[...].astype(f32)
    for g in range(group_count):
        for q in range(4):
            rows = slice(tokens * q, tokens * (q + 1))
            start = g * block + q * pack_width
            residual_pack[g, rows, : widths[q]] = residual[:, start : start + widths[q]]
            gain_pack[g, rows, : widths[q]] = jnp.broadcast_to(
                attn_gain[:, start : start + widths[q]], (tokens, widths[q])
            )
    square_acc[...] = jnp.zeros_like(square_acc)
    half_width = ROPE // 2
    at = lax.broadcasted_iota(jnp.int32, (tokens, half_width), 1).astype(f32)
    freqs = jnp.exp(at * (-2.0 / ROPE * math.log(10000.0)))
    angle = lengths_ref[...].astype(f32) * freqs
    rope_cos[...] = jnp.cos(angle)
    rope_sin[...] = jnp.sin(angle)

    for load in loads[:4]:
        load.wait()
    for t in range(tokens):
        query = q_lat[t]
        query_rope = q_rope[t]
        pages = [cache_lat[table_smem[t, p]] for p in range(PAGES_REQ)]
        scores = []
        for p in range(PAGES_REQ):
            rope_page = cache_rope[table_smem[t, p]]
            scores.append(
                lax.dot_general(
                    query, pages[p], (((1,), (1,)), ((), ())), preferred_element_type=f32
                )
                + jnp.dot(query_rope, rope_page, preferred_element_type=f32)
            )
        scores = jnp.concatenate(scores, axis=1) * score_scale
        live = lax.broadcasted_iota(jnp.int32, scores.shape, 1) < lengths_smem[t]
        masked = jnp.where(live, scores, -1e30)
        largest = jnp.max(masked, axis=1, keepdims=True)
        exps = jnp.where(live, jnp.exp(masked - largest), 0.0)
        attn_max[t] = largest
        attn_sum[t] = jnp.sum(exps, axis=1, keepdims=True)
        probs = exps.astype(bf16)
        summed = jnp.zeros((HEADS, LAT), f32)
        for p in range(PAGES_REQ):
            summed = summed + jnp.dot(
                probs[:, p * PAGE : (p + 1) * PAGE], pages[p], preferred_element_type=f32
            )
        attn_acc[t] = summed

    for r in range(1, dev_count):
        source = lax.rem(me_d + r, dev_count)
        remote(
            disp_send, disp_recv.at[source], disp_send_sem.at[r], disp_recv_sem.at[source], me_g, source
        ).wait_recv()
    for s in range(dev_count):
        part = disp_recv[s].astype(f32)
        for q in range(4):
            rows32[tokens * s : tokens * (s + 1), q * quarter : (q + 1) * quarter] = part[
                tokens * q : tokens * (q + 1), :
            ]
    for k in range(k_chunks):
        rows16[k] = rows32[:, k * k_rows : (k + 1) * k_rows].astype(bf16)

    gate_acc[...] = jnp.zeros_like(gate_acc)
    up_acc[...] = jnp.zeros_like(up_acc)

    @pl.loop(0, k_chunks)
    def _(k):
        gate_copy(k).wait()
        picked = rows16[k]
        gate_acc[...] += jnp.dot(picked, w_gate[k], preferred_element_type=f32)
        up_copy(k).wait()
        up_acc[...] += jnp.dot(picked, w_up[k], preferred_element_type=f32)

    gate_proj = gate_acc[...]
    hidden[...] = (gate_proj / (1.0 + jnp.exp(-gate_proj)) * up_acc[...]).astype(bf16)

    def ret_copy(step, r):
        dest = lax.rem(me_d + r, dev_count)
        return remote(
            ret_send.at[step, dest],
            ret_recv.at[step, me_d],
            ret_send_sem.at[step, r],
            ret_recv_sem.at[step, me_d],
            me_g,
            dest,
        )

    def col_copy(step, side):
        dest = chunk_at(step) * 2 + side
        return remote(
            col_send.at[step, side],
            col_recv.at[me_g],
            col_send_sem.at[step, side],
            col_recv_sem.at[me_g],
            dest,
            me_d,
        )

    def produce(step):
        down_copy(step).wait()
        result = jnp.dot(hidden[...], w_down[step], preferred_element_type=f32)
        for s in range(dev_count):
            for side in range(2):
                pieces = []
                for q in range(4):
                    start = side * block + q * pack_width
                    piece = result[tokens * s : tokens * (s + 1), start : start + widths[q]]
                    if widths[q] < pack_width:
                        piece = jnp.concatenate(
                            [piece, jnp.zeros((tokens, pack_width - widths[q]), f32)], axis=1
                        )
                    pieces.append(piece)
                ret_send[step, s, side] = jnp.concatenate(pieces, axis=0).astype(bf16)
        for r in range(1, dev_count):
            ret_copy(step, r).start()
        ret_recv[step, me_d] = ret_send[step, me_d]

    def consume(step):
        for r in range(1, dev_count):
            source = lax.rem(me_d + r, dev_count)
            remote(
                ret_send.at[step, source],
                ret_recv.at[step, source],
                ret_send_sem.at[step, r],
                ret_recv_sem.at[step, source],
                me_g,
                source,
            ).wait_recv()
        for side in range(2):
            g = chunk_at(step) * 2 + side
            total = residual_pack[g]
            moved = jnp.zeros_like(total)
            for e in range(dev_count):
                moved = moved + combine[e][:, :1] * ret_recv[step, e, side].astype(f32)
            following = (total + moved).astype(bf16).astype(f32)
            next_pack[g] = following
            square_acc[...] += following * following
            col_send[step, side] = (following * gain_pack[g]).astype(bf16)
        if step < chunks - 1:
            for side in range(2):
                col_copy(step, side).start()
        else:
            other = 1 - lax.rem(me_g, 2)
            col_copy(step, other).start()
            col_recv[me_g] = col_send[step, lax.rem(me_g, 2)]

    lag = 2
    for step in range(chunks):
        produce(step)
        if step >= lag:
            consume(step - lag)
    for step in range(max(chunks - lag, 0), chunks):
        consume(step)

    loads[4].wait()
    for r in range(1, group_count):
        source = lax.rem(me_g + r, group_count)
        remote(
            col_send.at[0, 0],
            col_recv.at[source],
            col_send_sem.at[0, 0],
            col_recv_sem.at[source],
            source,
            me_d,
        ).wait_recv()
    for g in range(group_count):
        part = col_recv[g].astype(f32)
        for q in range(4):
            col32[tokens * g : tokens * (g + 1), q * pack_width : q * pack_width + widths[q]] = part[
                tokens * q : tokens * (q + 1), : widths[q]
            ]
    partial = jnp.dot(col32[...].astype(bf16), w_kv[...], preferred_element_type=f32)
    for g in range(group_count):
        part_send[g] = partial[tokens * g : tokens * (g + 1), :]

    def part_copy(r):
        dest = lax.rem(me_g + r, group_count)
        return remote(
            part_send.at[dest],
            part_recv.at[me_g],
            part_send_sem.at[r],
            part_recv_sem.at[me_g],
            dest,
            me_d,
        )

    for r in range(1, group_count):
        part_copy(r).start()
    part_recv[me_g] = part_send[me_g]

    for g in range(group_count):
        part = next_pack[g]
        for q in range(4):
            start = g * block + q * pack_width
            next32[:, start : start + widths[q]] = part[tokens * q : tokens * (q + 1), : widths[q]]
    out_residual[...] = next32[...].astype(bf16)
    squares = jnp.sum(square_acc[...], axis=1, keepdims=True)
    squares = sum(squares[tokens * q : tokens * (q + 1)] for q in range(4))
    row_scale = lax.rsqrt(squares * (1.0 / width) + epsilon)

    for r in range(1, group_count):
        source = lax.rem(me_g + r, group_count)
        remote(
            part_send.at[source],
            part_recv.at[source],
            part_send_sem.at[r],
            part_recv_sem.at[source],
            source,
            me_d,
        ).wait_recv()
    kv_rows = part_recv[0]
    for g in range(1, group_count):
        kv_rows = kv_rows + part_recv[g]
    kv_rows = kv_rows * row_scale
    latent = kv_rows[:, :LAT]
    latent = (
        latent
        * lax.rsqrt(jnp.mean(latent * latent, axis=1, keepdims=True) + epsilon)
        * kv_gain_ref[...].astype(f32)
    ).astype(bf16)
    first_half = kv_rows[:, LAT : LAT + half_width]
    second_half = kv_rows[:, LAT + half_width :]
    cos, sin = rope_cos[...], rope_sin[...]
    rotated = jnp.concatenate(
        [first_half * cos - second_half * sin, second_half * cos + first_half * sin], axis=1
    ).astype(bf16)
    out_entry[:, :LAT] = latent
    out_entry[:, LAT:] = rotated
    latent = latent.astype(f32)
    rotated = rotated.astype(f32)
    for t in range(tokens):
        new_lat = latent[t : t + 1]
        self_score = (
            jnp.sum(q_lat[t].astype(f32) * new_lat, axis=1, keepdims=True)
            + jnp.sum(q_rope[t].astype(f32) * rotated[t : t + 1], axis=1, keepdims=True)
        ) * score_scale
        old = attn_max[t]
        largest = jnp.maximum(old, self_score)
        shrink = jnp.exp(old - largest)
        self_exp = jnp.exp(self_score - largest)
        inverse = 1.0 / (attn_sum[t] * shrink + self_exp)
        self_prob = self_exp.astype(bf16).astype(f32)
        out_attn[t] = (
            attn_acc[t] * (shrink * inverse) + (self_prob * inverse) * new_lat
        ).astype(bf16)

    for r in range(1, dev_count):
        disp_copy(r).wait_send()
        for step in range(chunks):
            ret_copy(step, r).wait_send()
    for step in range(chunks - 1):
        for side in range(2):
            col_copy(step, side).wait_send()
    col_copy(chunks - 1, 1 - lax.rem(me_g, 2)).wait_send()
    for r in range(1, group_count):
        part_copy(r).wait_send()


def fused(
    residual,
    routes,
    gate_weights,
    moe_gain,
    attn_gain,
    kv_gain,
    w_gate,
    w_up,
    w_down,
    w_kv,
    q_lat,
    q_rope,
    cache_lat,
    cache_rope,
    page_table,
    lengths,
):
    groups, devs = lax.axis_size("grp"), lax.axis_size("dev")
    tokens, width = residual.shape
    rows = tokens * devs
    units = w_gate.shape[1]
    chunks = groups // 2
    block = width // groups
    pack_width = -(-block // 512) * 128
    k_rows = 1024 if width % 1024 == 0 else width
    k_chunks = width // k_rows
    kv_width = w_kv.shape[1]
    f32, bf16 = jnp.float32, jnp.bfloat16
    vmem = pl.BlockSpec(memory_space=pltpu.VMEM)
    smem = pl.BlockSpec(memory_space=pltpu.SMEM)
    hbm = pl.BlockSpec(memory_space=pl.ANY)
    dma = pltpu.SemaphoreType.DMA
    scratch = [
        pltpu.VMEM((k_chunks, k_rows, units), bf16),
        pltpu.VMEM((k_chunks, k_rows, units), bf16),
        pltpu.VMEM((chunks, units, width // chunks), bf16),
        pltpu.VMEM(w_kv.shape, bf16),
        pltpu.VMEM(q_lat.shape, bf16),
        pltpu.VMEM(q_rope.shape, bf16),
        pltpu.VMEM(cache_lat.shape, bf16),
        pltpu.VMEM(cache_rope.shape, bf16),
        pltpu.VMEM((4 * tokens, width // 4), f32),
        pltpu.VMEM((4 * tokens, width // 4), bf16),
        pltpu.VMEM((devs, 4 * tokens, width // 4), bf16),
        pltpu.VMEM((rows, width), f32),
        pltpu.VMEM((k_chunks, rows, k_rows), bf16),
        pltpu.VMEM((rows, units), f32),
        pltpu.VMEM((rows, units), f32),
        pltpu.VMEM((rows, units), bf16),
        pltpu.VMEM((devs, 4 * tokens, 128), f32),
        pltpu.VMEM((groups, 4 * tokens, pack_width), f32),
        pltpu.VMEM((groups, 4 * tokens, pack_width), f32),
        pltpu.VMEM((groups, 4 * tokens, pack_width), f32),
        pltpu.VMEM((4 * tokens, pack_width), f32),
        pltpu.VMEM((chunks, devs, 2, 4 * tokens, pack_width), bf16),
        pltpu.VMEM((chunks, devs, 2, 4 * tokens, pack_width), bf16),
        pltpu.VMEM((chunks, 2, 4 * tokens, pack_width), bf16),
        pltpu.VMEM((groups, 4 * tokens, pack_width), bf16),
        pltpu.VMEM((groups * tokens, block), f32),
        pltpu.VMEM((groups, tokens, kv_width), f32),
        pltpu.VMEM((groups, tokens, kv_width), f32),
        pltpu.VMEM((tokens, HEADS, LAT), f32),
        pltpu.VMEM((tokens, HEADS, 1), f32),
        pltpu.VMEM((tokens, HEADS, 1), f32),
        pltpu.VMEM((tokens, ROPE // 2), f32),
        pltpu.VMEM((tokens, ROPE // 2), f32),
        pltpu.VMEM((tokens, width), f32),
        dma((5,)),
        dma((k_chunks,)),
        dma((k_chunks,)),
        dma((chunks,)),
        dma((devs,)),
        dma((devs,)),
        dma((chunks, devs)),
        dma((chunks, devs)),
        dma((chunks, 2)),
        dma((groups,)),
        dma((groups,)),
        dma((groups,)),
    ]
    return pl.pallas_call(
        functools.partial(fused_kernel, groups, devs),
        out_shape=(
            jax.ShapeDtypeStruct(residual.shape, bf16),
            jax.ShapeDtypeStruct((tokens, kv_width), bf16),
            jax.ShapeDtypeStruct(q_lat.shape, bf16),
        ),
        in_specs=[vmem] * 7 + [smem] * 2 + [hbm] * 8,
        out_specs=(vmem, vmem, vmem),
        scratch_shapes=scratch,
        compiler_params=pltpu.CompilerParams(
            collective_id=0, has_side_effects=True, vmem_limit_bytes=58 * 1024 * 1024
        ),
        cost_estimate=pl.CostEstimate(
            flops=1000000000, bytes_accessed=48000000, transcendentals=200000
        ),
    )(
        residual,
        routes,
        gate_weights,
        moe_gain.reshape(1, -1),
        attn_gain.reshape(1, -1),
        kv_gain.reshape(1, -1),
        lengths.reshape(-1, 1),
        lengths,
        page_table,
        w_gate,
        w_up,
        w_down,
        w_kv,
        q_lat,
        q_rope,
        cache_lat,
        cache_rope,
    )


def fits_fused(mesh):
    groups, devs = mesh.shape["grp"], mesh.shape["dev"]
    return devs == EXPERTS and groups % 2 == 0 and WIDTH % (128 * groups) == 0


def solution(mesh):
    body = fused if fits_fused(mesh) else local
    in_specs = (
        P(("grp", "dev"), None),
        P(("grp", "dev"), None),
        P(("grp", "dev"), None),
        P(),
        P(),
        P(),
        P(None, "dev"),
        P(None, "dev"),
        P("dev", None),
        P("grp", None),
        P(("grp", "dev"), None, None),
        P(("grp", "dev"), None, None),
        P(("grp", "dev"), None, None),
        P(("grp", "dev"), None, None),
        P(("grp", "dev"), None),
        P(("grp", "dev")),
    )
    out_specs = (P(("grp", "dev"), None), P(("grp", "dev"), None), P(("grp", "dev"), None, None))
    return jax.shard_map(body, mesh=mesh, in_specs=in_specs, out_specs=out_specs, check_vma=False)
```

```python
import functools
import math

import jax
import jax.numpy as jnp
from jax import lax
from jax.experimental import pallas as pl
from jax.experimental.pallas import tpu as pltpu
from jax.sharding import PartitionSpec as P

WIDTH = 7168
ATTEND_PLACES = (1, 2, 3, 4)
HEADS = 64
LAT = 512
ROPE = 64
EXPERTS = 4
TOP = 2
PAGE = 128
PAGES_REQ = 4
CAP = 3


epsilon = 1e-06
score_scale = 192.0 ** (-0.5)


def rms_scale(values, gain):
    widened = values.astype(jnp.float32)
    return (
        widened
        * lax.rsqrt(jnp.mean(widened * widened, axis=-1, keepdims=True) + epsilon)
        * gain.astype(jnp.float32)
    )


def expert_part(picked_rows, w_gate, w_up, w_down):
    gate_proj = jnp.dot(picked_rows, w_gate, preferred_element_type=jnp.float32)
    up_proj = jnp.dot(picked_rows, w_up, preferred_element_type=jnp.float32)
    hidden = (jax.nn.silu(gate_proj) * up_proj).astype(jnp.bfloat16)
    return jnp.dot(hidden, w_down, preferred_element_type=jnp.float32).astype(jnp.bfloat16)


def new_key(kv_rows, kv_gain, lengths):
    latent = rms_scale(kv_rows[:, :LAT], kv_gain)
    half_width = ROPE // 2
    freqs = 10000.0 ** (-(2.0 * jnp.arange(half_width, dtype=jnp.float32)) / ROPE)
    angle = lengths.astype(jnp.float32)[:, None] * freqs[None, :]
    first_half = kv_rows[:, LAT : LAT + half_width]
    second_half = kv_rows[:, LAT + half_width :]
    rotated = jnp.concatenate(
        [
            first_half * jnp.cos(angle) - second_half * jnp.sin(angle),
            second_half * jnp.cos(angle) + first_half * jnp.sin(angle),
        ],
        axis=1,
    )
    return jnp.concatenate([latent, rotated], axis=1).astype(jnp.bfloat16)


def attend(q_lat, q_rope, cache_lat, cache_rope, page_table, lengths, new_entry):
    token_count = q_lat.shape[0]
    key_span = PAGES_REQ * PAGE
    keys_lat = cache_lat[page_table].reshape(token_count, key_span, LAT)
    keys_rope = cache_rope[page_table]
    score_lat = jnp.einsum("thc,tlc->thl", q_lat, keys_lat, preferred_element_type=jnp.float32)
    score_rope = jnp.einsum(
        "thr,tpru->thpu", q_rope, keys_rope, preferred_element_type=jnp.float32
    ).reshape(token_count, HEADS, key_span)
    scores = (score_lat + score_rope) * score_scale
    new_lat = new_entry[:, :LAT]
    new_rope = new_entry[:, LAT:]
    self_score = (
        jnp.einsum("thc,tc->th", q_lat, new_lat, preferred_element_type=jnp.float32)
        + jnp.einsum("thr,tr->th", q_rope, new_rope, preferred_element_type=jnp.float32)
    ) * score_scale
    live_mask = (jnp.arange(key_span, dtype=jnp.int32)[None, :] < lengths[:, None])[:, None, :]
    masked = jnp.where(live_mask, scores, -1e30)
    largest = jnp.maximum(jnp.max(masked, axis=2), self_score)
    exps = jnp.where(live_mask, jnp.exp(masked - largest[:, :, None]), 0.0)
    self_exp = jnp.exp(self_score - largest)
    total = jnp.sum(exps, axis=2) + self_exp
    summed = jnp.einsum(
        "thl,tlc->thc", exps.astype(jnp.bfloat16), keys_lat, preferred_element_type=jnp.float32
    )
    self_prob = lax.optimization_barrier(self_exp.astype(jnp.bfloat16)).astype(jnp.float32)
    summed = summed + self_prob[:, :, None] * new_lat.astype(jnp.float32)[:, None, :]
    return (summed / total[:, :, None]).astype(jnp.bfloat16)


def local(
    residual,
    routes,
    gate_weights,
    moe_gain,
    attn_gain,
    kv_gain,
    w_gate,
    w_up,
    w_down,
    w_kv,
    q_lat,
    q_rope,
    cache_lat,
    cache_rope,
    page_table,
    lengths,
):
    token_count = residual.shape[0]
    moe_in = rms_scale(residual, moe_gain).astype(jnp.bfloat16)
    group_size = lax.axis_size("dev")
    shards = group_size // EXPERTS
    expert_ids = jnp.arange(EXPERTS, dtype=jnp.int32)
    flat_routes = routes.reshape(-1)
    onehot = (flat_routes[:, None] == expert_ids[None, :]).astype(jnp.int32)
    slot_index = jnp.sum((jnp.cumsum(onehot, axis=0) - onehot) * onehot, axis=1)
    picked = (
        (flat_routes[None, None, :] == expert_ids[:, None, None])
        & (slot_index[None, None, :] == jnp.arange(CAP, dtype=jnp.int32)[None, :, None])
    ).astype(jnp.float32)
    picked = picked.reshape(EXPERTS, CAP, token_count, TOP)
    placing = jnp.sum(picked, axis=3).astype(jnp.bfloat16)
    per_expert = jnp.einsum(
        "ect,td->ecd", placing, moe_in, preferred_element_type=jnp.float32
    ).astype(jnp.bfloat16)
    outgoing = jnp.repeat(per_expert, shards, axis=0)
    arrived = lax.all_to_all(outgoing, "dev", split_axis=0, concat_axis=0, tiled=True)
    sources, slot_count, feature_width = arrived.shape
    expert_rows = expert_part(
        arrived.reshape(sources * slot_count, feature_width), w_gate, w_up, w_down
    )
    returned = lax.all_to_all(
        expert_rows.reshape(sources, slot_count, feature_width),
        "dev",
        split_axis=0,
        concat_axis=0,
        tiled=True,
    )
    shard_sums = jnp.sum(returned.astype(jnp.float32).reshape(EXPERTS, shards, CAP, -1), axis=1)
    combine = jnp.einsum(
        "ectk,tk->tec", picked, gate_weights.astype(jnp.float32), precision=lax.Precision.HIGHEST
    )
    moe_out = jnp.einsum("tec,ecd->td", combine, shard_sums, precision=lax.Precision.HIGHEST)
    residual_next = (residual.astype(jnp.float32) + moe_out).astype(jnp.bfloat16)
    attn_in = rms_scale(residual_next, attn_gain).astype(jnp.bfloat16)
    column_rows = lax.all_to_all(attn_in, "grp", split_axis=1, concat_axis=0, tiled=True)
    kv_rows = lax.psum_scatter(
        jnp.dot(column_rows, w_kv, preferred_element_type=jnp.float32),
        "grp",
        scatter_dimension=0,
        tiled=True,
    )
    new_entry = new_key(kv_rows, kv_gain, lengths)
    attn_out = attend(q_lat, q_rope, cache_lat, cache_rope, page_table, lengths, new_entry)
    return (residual_next, new_entry, attn_out)


def fused_kernel(
    group_count,
    dev_count,
    residual_ref,
    routes_ref,
    gates_ref,
    moe_gain_ref,
    attn_gain_ref,
    kv_gain_ref,
    lengths_smem,
    table_smem,
    w_gate_hbm,
    w_up_hbm,
    w_down_hbm,
    w_kv_hbm,
    q_lat_hbm,
    q_rope_hbm,
    cache_lat_hbm,
    cache_rope_hbm,
    out_residual,
    out_entry,
    out_attn,
    w_gate,
    w_up,
    w_down,
    w_kv,
    q_lat,
    q_rope,
    cache_lat,
    cache_rope,
    pack32,
    disp_send,
    disp_recv,
    rows32,
    rows16,
    gate_acc,
    up_acc,
    hidden,
    combine,
    residual_pack,
    gain_pack,
    next_pack,
    square_acc,
    ret_send,
    ret_recv,
    col_send,
    col_recv,
    col32,
    part_send,
    part_recv,
    attn_acc,
    attn_max,
    attn_sum,
    rope_cos,
    rope_sin,
    next32,
    load_sem,
    gate_sem,
    up_sem,
    down_sem,
    disp_send_sem,
    disp_recv_sem,
    ret_send_sem,
    ret_recv_sem,
    col_send_sem,
    col_recv_sem,
    part_send_sem,
    part_recv_sem,
):
    f32 = jnp.float32
    bf16 = jnp.bfloat16
    me_g = lax.axis_index("grp")
    me_d = lax.axis_index("dev")
    tokens, width = residual_ref.shape
    quarter = width // 4
    chunks = group_count // 2
    block = width // group_count
    k_chunks, k_rows, _ = w_gate.shape
    down_cols = width // chunks
    pack_width = col_send.shape[-1]
    widths = [min(pack_width, block - q * pack_width) for q in range(4)]

    def remote(src, dst, send, recv, grp, dev):
        return pltpu.make_async_remote_copy(
            src_ref=src,
            dst_ref=dst,
            send_sem=send,
            recv_sem=recv,
            device_id=(grp, dev),
            device_id_type=pl.DeviceIdType.MESH,
        )

    barrier = pltpu.get_barrier_semaphore()
    for r in range(1, dev_count):
        pl.semaphore_signal(
            barrier,
            inc=1,
            device_id=(me_g, lax.rem(me_d + r, dev_count)),
            device_id_type=pl.DeviceIdType.MESH,
        )
    for r in range(1, group_count):
        pl.semaphore_signal(
            barrier,
            inc=1,
            device_id=(lax.rem(me_g + r, group_count), me_d),
            device_id_type=pl.DeviceIdType.MESH,
        )

    loads = [
        pltpu.make_async_copy(src, dst, load_sem.at[at])
        for at, (src, dst) in enumerate(
            [
                (q_lat_hbm, q_lat),
                (q_rope_hbm, q_rope),
                (cache_lat_hbm, cache_lat),
                (cache_rope_hbm, cache_rope),
                (w_kv_hbm, w_kv),
            ]
        )
    ]
    for load in loads[:4]:
        load.start()

    def gate_copy(k):
        return pltpu.make_async_copy(
            w_gate_hbm.at[pl.ds(k * k_rows, k_rows), :], w_gate.at[k], gate_sem.at[k]
        )

    def up_copy(k):
        return pltpu.make_async_copy(
            w_up_hbm.at[pl.ds(k * k_rows, k_rows), :], w_up.at[k], up_sem.at[k]
        )

    def chunk_at(step):
        return lax.rem(me_g // 2 + 1 + step, chunks)

    def down_copy(step):
        start = pl.multiple_of(chunk_at(step) * down_cols, 128)
        return pltpu.make_async_copy(
            w_down_hbm.at[:, pl.ds(start, down_cols)], w_down.at[step], down_sem.at[step]
        )

    for k in range(k_chunks):
        gate_copy(k).start()
        up_copy(k).start()
    for step in range(chunks):
        down_copy(step).start()
    loads[4].start()

    residual = residual_ref[...].astype(f32)
    moe_in = (
        residual
        * lax.rsqrt(jnp.mean(residual * residual, axis=1, keepdims=True) + epsilon)
    )
    moe_gain = moe_gain_ref[...].astype(f32)
    for q in range(4):
        for j in range(quarter // 128):
            lanes = q * (quarter // 128) + j
            pack32[tokens * q : tokens * (q + 1), j * 128 : (j + 1) * 128] = (
                moe_in[:, lanes * 128 : (lanes + 1) * 128] * moe_gain[lanes : lanes + 1]
            )
    packed = pack32[...].astype(bf16)
    disp_send[...] = packed
    disp_recv[me_d] = packed

    pl.semaphore_wait(barrier, dev_count - 1 + group_count - 1)

    def disp_copy(r):
        dest = lax.rem(me_d + r, dev_count)
        return remote(
            disp_send, disp_recv.at[me_d], disp_send_sem.at[r], disp_recv_sem.at[me_d], me_g, dest
        )

    for r in range(1, dev_count):
        disp_copy(r).start()

    routes = routes_ref[...]
    gates = gates_ref[...].astype(f32)
    diagonal = lax.broadcasted_iota(jnp.int32, (tokens, tokens), 0) == lax.broadcasted_iota(
        jnp.int32, (tokens, tokens), 1
    )
    for e in range(dev_count):
        weight = jnp.sum(jnp.where(routes == e, gates, 0.0), axis=0, keepdims=True)
        weight = jnp.sum(jnp.where(diagonal, weight, 0.0), axis=1, keepdims=True)
        weight = jnp.broadcast_to(weight, (tokens, 128))
        for q in range(4):
            combine[e, tokens * q : tokens * (q + 1), :] = weight
    residual_pack[...] = jnp.zeros_like(residual_pack)
    gain_pack[...] = jnp.zeros_like(gain_pack)
    attn_gain = attn_gain_ref[...].astype(f32)
    for g in range(group_count):
        for q in range(4):
            rows = slice(tokens * q, tokens * (q + 1))
            start = g * block + q * pack_width
            residual_pack[g, rows, : widths[q]] = residual[:, start : start + widths[q]]
            for j in range(widths[q] // 128):
                lanes = start // 128 + j
                gain_pack[g, rows, j * 128 : (j + 1) * 128] = jnp.broadcast_to(
                    attn_gain[lanes : lanes + 1], (tokens, 128)
                )
    square_acc[...] = jnp.zeros_like(square_acc)
    half_width = ROPE // 2
    at = lax.broadcasted_iota(jnp.int32, (tokens, half_width), 1).astype(f32)
    freqs = jnp.exp(at * (-2.0 / ROPE * math.log(10000.0)))
    row_at = lax.broadcasted_iota(jnp.int32, (tokens, half_width), 0)
    lengths = jnp.zeros((tokens, half_width), jnp.int32)
    for t in range(tokens):
        lengths = jnp.where(row_at == t, lengths_smem[t], lengths)
    angle = lengths.astype(f32) * freqs
    rope_cos[...] = jnp.cos(angle)
    rope_sin[...] = jnp.sin(angle)

    def attend_cached(t):
        query = q_lat[t]
        query_rope = q_rope[t]
        pages = [cache_lat[table_smem[t, p]] for p in range(PAGES_REQ)]
        scores = []
        for p in range(PAGES_REQ):
            rope_page = cache_rope[table_smem[t, p]]
            scores.append(
                lax.dot_general(
                    query, pages[p], (((1,), (1,)), ((), ())), preferred_element_type=f32
                )
                + jnp.dot(query_rope, rope_page, preferred_element_type=f32)
            )
        scores = jnp.concatenate(scores, axis=1) * score_scale
        live = lax.broadcasted_iota(jnp.int32, scores.shape, 1) < lengths_smem[t]
        masked = jnp.where(live, scores, -1e30)
        largest = jnp.max(masked, axis=1, keepdims=True)
        exps = jnp.where(live, jnp.exp(masked - largest), 0.0)
        attn_max[t] = largest
        attn_sum[t] = jnp.sum(exps, axis=1, keepdims=True)
        probs = exps.astype(bf16)
        summed = jnp.zeros((HEADS, LAT), f32)
        for p in range(PAGES_REQ):
            summed = summed + jnp.dot(
                probs[:, p * PAGE : (p + 1) * PAGE], pages[p], preferred_element_type=f32
            )
        attn_acc[t] = summed

    def attend_at(place):
        for t in range(tokens):
            if ATTEND_PLACES[t] == place:
                attend_cached(t)

    for load in loads[:4]:
        load.wait()
    attend_at(0)

    for r in range(1, dev_count):
        source = lax.rem(me_d + r, dev_count)
        remote(
            disp_send, disp_recv.at[source], disp_send_sem.at[r], disp_recv_sem.at[source], me_g, source
        ).wait_recv()
    for s in range(dev_count):
        part = disp_recv[s].astype(f32)
        for q in range(4):
            rows32[tokens * s : tokens * (s + 1), q * quarter : (q + 1) * quarter] = part[
                tokens * q : tokens * (q + 1), :
            ]
    for k in range(k_chunks):
        rows16[k] = rows32[:, k * k_rows : (k + 1) * k_rows].astype(bf16)

    gate_acc[...] = jnp.zeros_like(gate_acc)
    up_acc[...] = jnp.zeros_like(up_acc)

    @pl.loop(0, k_chunks)
    def _(k):
        gate_copy(k).wait()
        picked = rows16[k]
        gate_acc[...] += jnp.dot(picked, w_gate[k], preferred_element_type=f32)
        up_copy(k).wait()
        up_acc[...] += jnp.dot(picked, w_up[k], preferred_element_type=f32)

    gate_proj = gate_acc[...]
    hidden[...] = (gate_proj / (1.0 + jnp.exp(-gate_proj)) * up_acc[...]).astype(bf16)

    def ret_copy(step, r):
        dest = lax.rem(me_d + r, dev_count)
        return remote(
            ret_send.at[step, dest],
            ret_recv.at[step, me_d],
            ret_send_sem.at[step, r],
            ret_recv_sem.at[step, me_d],
            me_g,
            dest,
        )

    def col_copy(step, side):
        dest = chunk_at(step) * 2 + side
        return remote(
            col_send.at[step, side],
            col_recv.at[me_g],
            col_send_sem.at[step, side],
            col_recv_sem.at[me_g],
            dest,
            me_d,
        )

    def produce(step):
        down_copy(step).wait()
        result = jnp.dot(hidden[...], w_down[step], preferred_element_type=f32)
        for s in range(dev_count):
            for side in range(2):
                pieces = []
                for q in range(4):
                    start = side * block + q * pack_width
                    piece = result[tokens * s : tokens * (s + 1), start : start + widths[q]]
                    if widths[q] < pack_width:
                        piece = jnp.concatenate(
                            [piece, jnp.zeros((tokens, pack_width - widths[q]), f32)], axis=1
                        )
                    pieces.append(piece)
                ret_send[step, s, side] = jnp.concatenate(pieces, axis=0).astype(bf16)
        for r in range(1, dev_count):
            ret_copy(step, r).start()
        ret_recv[step, me_d] = ret_send[step, me_d]

    def consume(step):
        for r in range(1, dev_count):
            source = lax.rem(me_d + r, dev_count)
            remote(
                ret_send.at[step, source],
                ret_recv.at[step, source],
                ret_send_sem.at[step, r],
                ret_recv_sem.at[step, source],
                me_g,
                source,
            ).wait_recv()
        for side in range(2):
            g = chunk_at(step) * 2 + side
            total = residual_pack[g]
            moved = jnp.zeros_like(total)
            for e in range(dev_count):
                moved = moved + combine[e][:, :1] * ret_recv[step, e, side].astype(f32)
            following = (total + moved).astype(bf16).astype(f32)
            next_pack[g] = following
            square_acc[...] += following * following
            col_send[step, side] = (following * gain_pack[g]).astype(bf16)
        if step < chunks - 1:
            for side in range(2):
                col_copy(step, side).start()
        else:
            other = 1 - lax.rem(me_g, 2)
            col_copy(step, other).start()
            col_recv[me_g] = col_send[step, lax.rem(me_g, 2)]

    lag = 2
    for step in range(chunks):
        produce(step)
        if step >= lag:
            consume(step - lag)
    for step in range(max(chunks - lag, 0), chunks):
        attend_at(1 if step < chunks - 1 else 2)
        consume(step)
    attend_at(3)

    loads[4].wait()
    for r in range(1, group_count):
        source = lax.rem(me_g + r, group_count)
        remote(
            col_send.at[0, 0],
            col_recv.at[source],
            col_send_sem.at[0, 0],
            col_recv_sem.at[source],
            source,
            me_d,
        ).wait_recv()
    for g in range(group_count):
        part = col_recv[g].astype(f32)
        for q in range(4):
            col32[tokens * g : tokens * (g + 1), q * pack_width : q * pack_width + widths[q]] = part[
                tokens * q : tokens * (q + 1), : widths[q]
            ]
    partial = lax.dot_general(
        col32[...].astype(bf16), w_kv[...], (((1,), (1,)), ((), ())), preferred_element_type=f32
    )
    for g in range(group_count):
        part_send[g] = partial[tokens * g : tokens * (g + 1), :]

    def part_copy(r):
        dest = lax.rem(me_g + r, group_count)
        return remote(
            part_send.at[dest],
            part_recv.at[me_g],
            part_send_sem.at[r],
            part_recv_sem.at[me_g],
            dest,
            me_d,
        )

    for r in range(1, group_count):
        part_copy(r).start()
    part_recv[me_g] = part_send[me_g]
    attend_at(4)

    for g in range(group_count):
        part = next_pack[g]
        for q in range(4):
            start = g * block + q * pack_width
            next32[:, start : start + widths[q]] = part[tokens * q : tokens * (q + 1), : widths[q]]
    out_residual[...] = next32[...].astype(bf16)
    squares = jnp.sum(square_acc[...], axis=1, keepdims=True)
    squares = sum(squares[tokens * q : tokens * (q + 1)] for q in range(4))
    row_scale = lax.rsqrt(squares * (1.0 / width) + epsilon)

    for r in range(1, group_count):
        source = lax.rem(me_g + r, group_count)
        remote(
            part_send.at[source],
            part_recv.at[source],
            part_send_sem.at[r],
            part_recv_sem.at[source],
            source,
            me_d,
        ).wait_recv()
    kv_rows = part_recv[0]
    for g in range(1, group_count):
        kv_rows = kv_rows + part_recv[g]
    kv_rows = kv_rows * row_scale
    latent = kv_rows[:, :LAT]
    latent = latent * lax.rsqrt(jnp.mean(latent * latent, axis=1, keepdims=True) + epsilon)
    kv_gain = kv_gain_ref[...].astype(f32)
    latent = jnp.concatenate(
        [latent[:, j * 128 : (j + 1) * 128] * kv_gain[j : j + 1] for j in range(LAT // 128)],
        axis=1,
    ).astype(bf16)
    first_half = kv_rows[:, LAT : LAT + half_width]
    second_half = kv_rows[:, LAT + half_width :]
    cos, sin = rope_cos[...], rope_sin[...]
    rotated = jnp.concatenate(
        [first_half * cos - second_half * sin, second_half * cos + first_half * sin], axis=1
    ).astype(bf16)
    out_entry[:, :LAT] = latent
    out_entry[:, LAT:] = rotated
    latent = latent.astype(f32)
    rotated = rotated.astype(f32)
    for t in range(tokens):
        new_lat = latent[t : t + 1]
        self_score = (
            jnp.sum(q_lat[t].astype(f32) * new_lat, axis=1, keepdims=True)
            + jnp.sum(q_rope[t].astype(f32) * rotated[t : t + 1], axis=1, keepdims=True)
        ) * score_scale
        old = attn_max[t]
        largest = jnp.maximum(old, self_score)
        shrink = jnp.exp(old - largest)
        self_exp = jnp.exp(self_score - largest)
        inverse = 1.0 / (attn_sum[t] * shrink + self_exp)
        self_prob = self_exp.astype(bf16).astype(f32)
        out_attn[t] = (
            attn_acc[t] * (shrink * inverse) + (self_prob * inverse) * new_lat
        ).astype(bf16)

    for r in range(1, dev_count):
        disp_copy(r).wait_send()
        for step in range(chunks):
            ret_copy(step, r).wait_send()
    for step in range(chunks - 1):
        for side in range(2):
            col_copy(step, side).wait_send()
    col_copy(chunks - 1, 1 - lax.rem(me_g, 2)).wait_send()
    for r in range(1, group_count):
        part_copy(r).wait_send()


def fused(
    residual,
    routes,
    gate_weights,
    moe_gain,
    attn_gain,
    kv_gain,
    w_gate,
    w_up,
    w_down,
    w_kv,
    q_lat,
    q_rope,
    cache_lat,
    cache_rope,
    page_table,
    lengths,
):
    groups, devs = lax.axis_size("grp"), lax.axis_size("dev")
    tokens, width = residual.shape
    rows = tokens * devs
    units = w_gate.shape[1]
    chunks = groups // 2
    block = width // groups
    pack_width = -(-block // 512) * 128
    k_rows = 1024 if width % 1024 == 0 else width
    k_chunks = width // k_rows
    w_kv = w_kv.T
    kv_width = w_kv.shape[0]
    f32, bf16 = jnp.float32, jnp.bfloat16
    vmem = pl.BlockSpec(memory_space=pltpu.VMEM)
    smem = pl.BlockSpec(memory_space=pltpu.SMEM)
    hbm = pl.BlockSpec(memory_space=pl.ANY)
    dma = pltpu.SemaphoreType.DMA
    scratch = [
        pltpu.VMEM((k_chunks, k_rows, units), bf16),
        pltpu.VMEM((k_chunks, k_rows, units), bf16),
        pltpu.VMEM((chunks, units, width // chunks), bf16),
        pltpu.VMEM(w_kv.shape, bf16),
        pltpu.VMEM(q_lat.shape, bf16),
        pltpu.VMEM(q_rope.shape, bf16),
        pltpu.VMEM(cache_lat.shape, bf16),
        pltpu.VMEM(cache_rope.shape, bf16),
        pltpu.VMEM((4 * tokens, width // 4), f32),
        pltpu.VMEM((4 * tokens, width // 4), bf16),
        pltpu.VMEM((devs, 4 * tokens, width // 4), bf16),
        pltpu.VMEM((rows, width), f32),
        pltpu.VMEM((k_chunks, rows, k_rows), bf16),
        pltpu.VMEM((rows, units), f32),
        pltpu.VMEM((rows, units), f32),
        pltpu.VMEM((rows, units), bf16),
        pltpu.VMEM((devs, 4 * tokens, 128), f32),
        pltpu.VMEM((groups, 4 * tokens, pack_width), f32),
        pltpu.VMEM((groups, 4 * tokens, pack_width), f32),
        pltpu.VMEM((groups, 4 * tokens, pack_width), f32),
        pltpu.VMEM((4 * tokens, pack_width), f32),
        pltpu.VMEM((chunks, devs, 2, 4 * tokens, pack_width), bf16),
        pltpu.VMEM((chunks, devs, 2, 4 * tokens, pack_width), bf16),
        pltpu.VMEM((chunks, 2, 4 * tokens, pack_width), bf16),
        pltpu.VMEM((groups, 4 * tokens, pack_width), bf16),
        pltpu.VMEM((groups * tokens, block), f32),
        pltpu.VMEM((groups, tokens, kv_width), f32),
        pltpu.VMEM((groups, tokens, kv_width), f32),
        pltpu.VMEM((tokens, HEADS, LAT), f32),
        pltpu.VMEM((tokens, HEADS, 1), f32),
        pltpu.VMEM((tokens, HEADS, 1), f32),
        pltpu.VMEM((tokens, ROPE // 2), f32),
        pltpu.VMEM((tokens, ROPE // 2), f32),
        pltpu.VMEM((tokens, width), f32),
        dma((5,)),
        dma((k_chunks,)),
        dma((k_chunks,)),
        dma((chunks,)),
        dma((devs,)),
        dma((devs,)),
        dma((chunks, devs)),
        dma((chunks, devs)),
        dma((chunks, 2)),
        dma((groups,)),
        dma((groups,)),
        dma((groups,)),
    ]
    results = pl.pallas_call(
        functools.partial(fused_kernel, groups, devs),
        out_shape=(
            jax.ShapeDtypeStruct(residual.shape, bf16),
            jax.ShapeDtypeStruct((tokens, kv_width), bf16),
            jax.ShapeDtypeStruct(q_lat.shape, bf16),
        ),
        in_specs=[vmem] * 6 + [smem] * 2 + [hbm] * 8,
        out_specs=(vmem, vmem, vmem),
        scratch_shapes=scratch,
        compiler_params=pltpu.CompilerParams(
            collective_id=0, has_side_effects=True, vmem_limit_bytes=58 * 1024 * 1024
        ),
        cost_estimate=pl.CostEstimate(
            flops=1000000000, bytes_accessed=48000000, transcendentals=200000
        ),
    )(
        residual,
        routes.T,
        gate_weights.T,
        moe_gain.reshape(-1, 128),
        attn_gain.reshape(-1, 128),
        kv_gain.reshape(-1, 128),
        lengths,
        page_table,
        w_gate,
        w_up,
        w_down,
        w_kv,
        q_lat,
        q_rope,
        cache_lat,
        cache_rope,
    )
    return pl.pallas_call(
        copy_kernel,
        out_shape=tuple(jax.ShapeDtypeStruct(one.shape, one.dtype) for one in results),
        in_specs=[vmem] * 3,
        out_specs=(vmem,) * 3,
    )(*results)


def copy_kernel(residual_in, entry_in, attn_in, residual_out, entry_out, attn_out):
    residual_out[...] = residual_in[...]
    entry_out[...] = entry_in[...]
    attn_out[...] = attn_in[...]


def fits_fused(mesh):
    groups, devs = mesh.shape["grp"], mesh.shape["dev"]
    return devs == EXPERTS and groups % 2 == 0 and WIDTH % (128 * groups) == 0


def solution(mesh):
    body = fused if fits_fused(mesh) else local
    in_specs = (
        P(("grp", "dev"), None),
        P(("grp", "dev"), None),
        P(("grp", "dev"), None),
        P(),
        P(),
        P(),
        P(None, "dev"),
        P(None, "dev"),
        P("dev", None),
        P("grp", None),
        P(("grp", "dev"), None, None),
        P(("grp", "dev"), None, None),
        P(("grp", "dev"), None, None),
        P(("grp", "dev"), None, None),
        P(("grp", "dev"), None),
        P(("grp", "dev")),
    )
    out_specs = (P(("grp", "dev"), None), P(("grp", "dev"), None), P(("grp", "dev"), None, None))
    return jax.shard_map(body, mesh=mesh, in_specs=in_specs, out_specs=out_specs, check_vma=False)
```

```python
import functools
import math

import jax
import jax.numpy as jnp
from jax import lax
from jax.experimental import pallas as pl
from jax.experimental.pallas import tpu as pltpu
from jax.sharding import PartitionSpec as P

WIDTH = 7168
K_STEPS = 2
ATTEND_PLACES = (1, 2, 3, 4)
HEADS = 64
LAT = 512
ROPE = 64
EXPERTS = 4
TOP = 2
PAGE = 128
PAGES_REQ = 4
CAP = 3


epsilon = 1e-06
score_scale = 192.0 ** (-0.5)


def rms_scale(values, gain):
    widened = values.astype(jnp.float32)
    return (
        widened
        * lax.rsqrt(jnp.mean(widened * widened, axis=-1, keepdims=True) + epsilon)
        * gain.astype(jnp.float32)
    )


def expert_part(picked_rows, w_gate, w_up, w_down):
    gate_proj = jnp.dot(picked_rows, w_gate, preferred_element_type=jnp.float32)
    up_proj = jnp.dot(picked_rows, w_up, preferred_element_type=jnp.float32)
    hidden = (jax.nn.silu(gate_proj) * up_proj).astype(jnp.bfloat16)
    return jnp.dot(hidden, w_down, preferred_element_type=jnp.float32).astype(jnp.bfloat16)


def new_key(kv_rows, kv_gain, lengths):
    latent = rms_scale(kv_rows[:, :LAT], kv_gain)
    half_width = ROPE // 2
    freqs = 10000.0 ** (-(2.0 * jnp.arange(half_width, dtype=jnp.float32)) / ROPE)
    angle = lengths.astype(jnp.float32)[:, None] * freqs[None, :]
    first_half = kv_rows[:, LAT : LAT + half_width]
    second_half = kv_rows[:, LAT + half_width :]
    rotated = jnp.concatenate(
        [
            first_half * jnp.cos(angle) - second_half * jnp.sin(angle),
            second_half * jnp.cos(angle) + first_half * jnp.sin(angle),
        ],
        axis=1,
    )
    return jnp.concatenate([latent, rotated], axis=1).astype(jnp.bfloat16)


def attend(q_lat, q_rope, cache_lat, cache_rope, page_table, lengths, new_entry):
    token_count = q_lat.shape[0]
    key_span = PAGES_REQ * PAGE
    keys_lat = cache_lat[page_table].reshape(token_count, key_span, LAT)
    keys_rope = cache_rope[page_table]
    score_lat = jnp.einsum("thc,tlc->thl", q_lat, keys_lat, preferred_element_type=jnp.float32)
    score_rope = jnp.einsum(
        "thr,tpru->thpu", q_rope, keys_rope, preferred_element_type=jnp.float32
    ).reshape(token_count, HEADS, key_span)
    scores = (score_lat + score_rope) * score_scale
    new_lat = new_entry[:, :LAT]
    new_rope = new_entry[:, LAT:]
    self_score = (
        jnp.einsum("thc,tc->th", q_lat, new_lat, preferred_element_type=jnp.float32)
        + jnp.einsum("thr,tr->th", q_rope, new_rope, preferred_element_type=jnp.float32)
    ) * score_scale
    live_mask = (jnp.arange(key_span, dtype=jnp.int32)[None, :] < lengths[:, None])[:, None, :]
    masked = jnp.where(live_mask, scores, -1e30)
    largest = jnp.maximum(jnp.max(masked, axis=2), self_score)
    exps = jnp.where(live_mask, jnp.exp(masked - largest[:, :, None]), 0.0)
    self_exp = jnp.exp(self_score - largest)
    total = jnp.sum(exps, axis=2) + self_exp
    summed = jnp.einsum(
        "thl,tlc->thc", exps.astype(jnp.bfloat16), keys_lat, preferred_element_type=jnp.float32
    )
    self_prob = lax.optimization_barrier(self_exp.astype(jnp.bfloat16)).astype(jnp.float32)
    summed = summed + self_prob[:, :, None] * new_lat.astype(jnp.float32)[:, None, :]
    return (summed / total[:, :, None]).astype(jnp.bfloat16)


def local(
    residual,
    routes,
    gate_weights,
    moe_gain,
    attn_gain,
    kv_gain,
    w_gate,
    w_up,
    w_down,
    w_kv,
    q_lat,
    q_rope,
    cache_lat,
    cache_rope,
    page_table,
    lengths,
):
    token_count = residual.shape[0]
    moe_in = rms_scale(residual, moe_gain).astype(jnp.bfloat16)
    group_size = lax.axis_size("dev")
    shards = group_size // EXPERTS
    expert_ids = jnp.arange(EXPERTS, dtype=jnp.int32)
    flat_routes = routes.reshape(-1)
    onehot = (flat_routes[:, None] == expert_ids[None, :]).astype(jnp.int32)
    slot_index = jnp.sum((jnp.cumsum(onehot, axis=0) - onehot) * onehot, axis=1)
    picked = (
        (flat_routes[None, None, :] == expert_ids[:, None, None])
        & (slot_index[None, None, :] == jnp.arange(CAP, dtype=jnp.int32)[None, :, None])
    ).astype(jnp.float32)
    picked = picked.reshape(EXPERTS, CAP, token_count, TOP)
    placing = jnp.sum(picked, axis=3).astype(jnp.bfloat16)
    per_expert = jnp.einsum(
        "ect,td->ecd", placing, moe_in, preferred_element_type=jnp.float32
    ).astype(jnp.bfloat16)
    outgoing = jnp.repeat(per_expert, shards, axis=0)
    arrived = lax.all_to_all(outgoing, "dev", split_axis=0, concat_axis=0, tiled=True)
    sources, slot_count, feature_width = arrived.shape
    expert_rows = expert_part(
        arrived.reshape(sources * slot_count, feature_width), w_gate, w_up, w_down
    )
    returned = lax.all_to_all(
        expert_rows.reshape(sources, slot_count, feature_width),
        "dev",
        split_axis=0,
        concat_axis=0,
        tiled=True,
    )
    shard_sums = jnp.sum(returned.astype(jnp.float32).reshape(EXPERTS, shards, CAP, -1), axis=1)
    combine = jnp.einsum(
        "ectk,tk->tec", picked, gate_weights.astype(jnp.float32), precision=lax.Precision.HIGHEST
    )
    moe_out = jnp.einsum("tec,ecd->td", combine, shard_sums, precision=lax.Precision.HIGHEST)
    residual_next = (residual.astype(jnp.float32) + moe_out).astype(jnp.bfloat16)
    attn_in = rms_scale(residual_next, attn_gain).astype(jnp.bfloat16)
    column_rows = lax.all_to_all(attn_in, "grp", split_axis=1, concat_axis=0, tiled=True)
    kv_rows = lax.psum_scatter(
        jnp.dot(column_rows, w_kv, preferred_element_type=jnp.float32),
        "grp",
        scatter_dimension=0,
        tiled=True,
    )
    new_entry = new_key(kv_rows, kv_gain, lengths)
    attn_out = attend(q_lat, q_rope, cache_lat, cache_rope, page_table, lengths, new_entry)
    return (residual_next, new_entry, attn_out)


def fused_kernel(
    group_count,
    dev_count,
    residual_ref,
    routes_ref,
    gates_ref,
    moe_gain_ref,
    attn_gain_ref,
    kv_gain_ref,
    lengths_smem,
    table_smem,
    w_gate_hbm,
    w_up_hbm,
    w_down_hbm,
    w_kv_hbm,
    q_lat_hbm,
    q_rope_hbm,
    cache_lat_hbm,
    cache_rope_hbm,
    out_residual,
    out_entry,
    out_attn,
    w_gate,
    w_up,
    w_down,
    w_kv,
    q_lat,
    q_rope,
    cache_lat,
    cache_rope,
    pack32,
    disp_send,
    disp_recv,
    rows32,
    rows16,
    gate_acc,
    up_acc,
    hidden,
    combine,
    residual_pack,
    gain_pack,
    next_pack,
    square_acc,
    ret_send,
    ret_recv,
    col_send,
    col_recv,
    col32,
    part_send,
    part_recv,
    attn_acc,
    attn_max,
    attn_sum,
    rope_cos,
    rope_sin,
    next32,
    load_sem,
    gate_sem,
    up_sem,
    down_sem,
    disp_send_sem,
    disp_recv_sem,
    ret_send_sem,
    ret_recv_sem,
    col_send_sem,
    col_recv_sem,
    part_send_sem,
    part_recv_sem,
):
    f32 = jnp.float32
    bf16 = jnp.bfloat16
    me_g = lax.axis_index("grp")
    me_d = lax.axis_index("dev")
    tokens, width = residual_ref.shape
    piece = width // 8
    chunks = group_count // 2
    block = width // group_count
    k_chunks, k_rows, _ = w_gate.shape
    down_cols = width // chunks
    pack_width = col_send.shape[-1]
    widths = [min(pack_width, block - q * pack_width) for q in range(4)]

    def remote(src, dst, send, recv, grp, dev):
        return pltpu.make_async_remote_copy(
            src_ref=src,
            dst_ref=dst,
            send_sem=send,
            recv_sem=recv,
            device_id=(grp, dev),
            device_id_type=pl.DeviceIdType.MESH,
        )

    barrier = pltpu.get_barrier_semaphore()
    for r in range(1, dev_count):
        pl.semaphore_signal(
            barrier,
            inc=1,
            device_id=(me_g, lax.rem(me_d + r, dev_count)),
            device_id_type=pl.DeviceIdType.MESH,
        )
    for r in range(1, group_count):
        pl.semaphore_signal(
            barrier,
            inc=1,
            device_id=(lax.rem(me_g + r, group_count), me_d),
            device_id_type=pl.DeviceIdType.MESH,
        )

    loads = [
        pltpu.make_async_copy(src, dst, load_sem.at[at])
        for at, (src, dst) in enumerate(
            [
                (q_lat_hbm, q_lat),
                (q_rope_hbm, q_rope),
                (cache_lat_hbm, cache_lat),
                (cache_rope_hbm, cache_rope),
                (w_kv_hbm, w_kv),
            ]
        )
    ]
    for load in loads[:4]:
        load.start()

    def gate_copy(k):
        return pltpu.make_async_copy(
            w_gate_hbm.at[pl.ds(k * k_rows, k_rows), :], w_gate.at[k], gate_sem.at[k]
        )

    def up_copy(k):
        return pltpu.make_async_copy(
            w_up_hbm.at[pl.ds(k * k_rows, k_rows), :], w_up.at[k], up_sem.at[k]
        )

    def chunk_at(step):
        return lax.rem(me_g // 2 + 1 + step, chunks)

    def down_copy(step):
        start = pl.multiple_of(chunk_at(step) * down_cols, 128)
        return pltpu.make_async_copy(
            w_down_hbm.at[:, pl.ds(start, down_cols)], w_down.at[step], down_sem.at[step]
        )

    for k in range(k_chunks):
        gate_copy(k).start()
        up_copy(k).start()
    for step in range(chunks):
        down_copy(step).start()
    loads[4].start()

    residual = residual_ref[...].astype(f32)
    moe_in = (
        residual
        * lax.rsqrt(jnp.mean(residual * residual, axis=1, keepdims=True) + epsilon)
    )
    moe_gain = moe_gain_ref[...].astype(f32)
    for half in range(2):
        for q in range(4):
            for j in range(piece // 128):
                lanes = (half * 4 + q) * (piece // 128) + j
                pack32[half, tokens * q : tokens * (q + 1), j * 128 : (j + 1) * 128] = (
                    moe_in[:, lanes * 128 : (lanes + 1) * 128] * moe_gain[lanes : lanes + 1]
                )
    packed = pack32[...].astype(bf16)
    disp_send[...] = packed
    for half in range(2):
        disp_recv[half, me_d] = packed[half]

    pl.semaphore_wait(barrier, dev_count - 1 + group_count - 1)

    def disp_copy(half, r):
        dest = lax.rem(me_d + r, dev_count)
        return remote(
            disp_send.at[half],
            disp_recv.at[half, me_d],
            disp_send_sem.at[half, r],
            disp_recv_sem.at[half, me_d],
            me_g,
            dest,
        )

    for half in range(2):
        for r in range(1, dev_count):
            disp_copy(half, r).start()

    routes = routes_ref[...]
    gates = gates_ref[...].astype(f32)
    diagonal = lax.broadcasted_iota(jnp.int32, (tokens, tokens), 0) == lax.broadcasted_iota(
        jnp.int32, (tokens, tokens), 1
    )
    for e in range(dev_count):
        weight = jnp.sum(jnp.where(routes == e, gates, 0.0), axis=0, keepdims=True)
        weight = jnp.sum(jnp.where(diagonal, weight, 0.0), axis=1, keepdims=True)
        weight = jnp.broadcast_to(weight, (tokens, 128))
        for q in range(4):
            combine[e, tokens * q : tokens * (q + 1), :] = weight
    residual_pack[...] = jnp.zeros_like(residual_pack)
    gain_pack[...] = jnp.zeros_like(gain_pack)
    attn_gain = attn_gain_ref[...].astype(f32)
    for g in range(group_count):
        for q in range(4):
            rows = slice(tokens * q, tokens * (q + 1))
            start = g * block + q * pack_width
            residual_pack[g, rows, : widths[q]] = residual[:, start : start + widths[q]]
            for j in range(widths[q] // 128):
                lanes = start // 128 + j
                gain_pack[g, rows, j * 128 : (j + 1) * 128] = jnp.broadcast_to(
                    attn_gain[lanes : lanes + 1], (tokens, 128)
                )
    square_acc[...] = jnp.zeros_like(square_acc)
    half_width = ROPE // 2
    at = lax.broadcasted_iota(jnp.int32, (tokens, half_width), 1).astype(f32)
    freqs = jnp.exp(at * (-2.0 / ROPE * math.log(10000.0)))
    row_at = lax.broadcasted_iota(jnp.int32, (tokens, half_width), 0)
    lengths = jnp.zeros((tokens, half_width), jnp.int32)
    for t in range(tokens):
        lengths = jnp.where(row_at == t, lengths_smem[t], lengths)
    angle = lengths.astype(f32) * freqs
    rope_cos[...] = jnp.cos(angle)
    rope_sin[...] = jnp.sin(angle)

    def attend_cached(t):
        query = q_lat[t]
        query_rope = q_rope[t]
        pages = [cache_lat[table_smem[t, p]] for p in range(PAGES_REQ)]
        scores = []
        for p in range(PAGES_REQ):
            rope_page = cache_rope[table_smem[t, p]]
            scores.append(
                lax.dot_general(
                    query, pages[p], (((1,), (1,)), ((), ())), preferred_element_type=f32
                )
                + jnp.dot(query_rope, rope_page, preferred_element_type=f32)
            )
        scores = jnp.concatenate(scores, axis=1) * score_scale
        live = lax.broadcasted_iota(jnp.int32, scores.shape, 1) < lengths_smem[t]
        masked = jnp.where(live, scores, -1e30)
        largest = jnp.max(masked, axis=1, keepdims=True)
        exps = jnp.where(live, jnp.exp(masked - largest), 0.0)
        attn_max[t] = largest
        attn_sum[t] = jnp.sum(exps, axis=1, keepdims=True)
        probs = exps.astype(bf16)
        summed = jnp.zeros((HEADS, LAT), f32)
        for p in range(PAGES_REQ):
            summed = summed + jnp.dot(
                probs[:, p * PAGE : (p + 1) * PAGE], pages[p], preferred_element_type=f32
            )
        attn_acc[t] = summed

    def attend_at(place):
        for t in range(tokens):
            if ATTEND_PLACES[t] == place:
                attend_cached(t)

    for load in loads[:4]:
        load.wait()
    attend_at(0)

    gate_acc[...] = jnp.zeros_like(gate_acc)
    up_acc[...] = jnp.zeros_like(up_acc)
    half_chunks = k_chunks // 2
    for half in range(2):
        for r in range(1, dev_count):
            source = lax.rem(me_d + r, dev_count)
            remote(
                disp_send.at[half],
                disp_recv.at[half, source],
                disp_send_sem.at[half, r],
                disp_recv_sem.at[half, source],
                me_g,
                source,
            ).wait_recv()
        for s in range(dev_count):
            part = disp_recv[half, s].astype(f32)
            for q in range(4):
                rows32[tokens * s : tokens * (s + 1), q * piece : (q + 1) * piece] = part[
                    tokens * q : tokens * (q + 1), :
                ]
        for k in range(half_chunks):
            rows16[half * half_chunks + k] = rows32[:, k * k_rows : (k + 1) * k_rows].astype(bf16)

        @pl.loop(half * half_chunks, (half + 1) * half_chunks)
        def _(k):
            gate_copy(k).wait()
            picked = rows16[k]
            gate_acc[...] += jnp.dot(picked, w_gate[k], preferred_element_type=f32)
            up_copy(k).wait()
            up_acc[...] += jnp.dot(picked, w_up[k], preferred_element_type=f32)

    gate_proj = gate_acc[...]
    hidden[...] = (gate_proj / (1.0 + jnp.exp(-gate_proj)) * up_acc[...]).astype(bf16)

    def ret_copy(step, r):
        dest = lax.rem(me_d + r, dev_count)
        return remote(
            ret_send.at[step, dest],
            ret_recv.at[step, me_d],
            ret_send_sem.at[step, r],
            ret_recv_sem.at[step, me_d],
            me_g,
            dest,
        )

    def col_copy(step, side):
        dest = chunk_at(step) * 2 + side
        return remote(
            col_send.at[step, side],
            col_recv.at[me_g],
            col_send_sem.at[step, side],
            col_recv_sem.at[me_g],
            dest,
            me_d,
        )

    def produce(step):
        down_copy(step).wait()
        result = jnp.dot(hidden[...], w_down[step], preferred_element_type=f32)
        for s in range(dev_count):
            for side in range(2):
                pieces = []
                for q in range(4):
                    start = side * block + q * pack_width
                    piece = result[tokens * s : tokens * (s + 1), start : start + widths[q]]
                    if widths[q] < pack_width:
                        piece = jnp.concatenate(
                            [piece, jnp.zeros((tokens, pack_width - widths[q]), f32)], axis=1
                        )
                    pieces.append(piece)
                ret_send[step, s, side] = jnp.concatenate(pieces, axis=0).astype(bf16)
        for r in range(1, dev_count):
            ret_copy(step, r).start()
        ret_recv[step, me_d] = ret_send[step, me_d]

    def consume(step):
        for r in range(1, dev_count):
            source = lax.rem(me_d + r, dev_count)
            remote(
                ret_send.at[step, source],
                ret_recv.at[step, source],
                ret_send_sem.at[step, r],
                ret_recv_sem.at[step, source],
                me_g,
                source,
            ).wait_recv()
        for side in range(2):
            g = chunk_at(step) * 2 + side
            total = residual_pack[g]
            moved = jnp.zeros_like(total)
            for e in range(dev_count):
                moved = moved + combine[e][:, :1] * ret_recv[step, e, side].astype(f32)
            following = (total + moved).astype(bf16).astype(f32)
            next_pack[g] = following
            square_acc[...] += following * following
            col_send[step, side] = (following * gain_pack[g]).astype(bf16)
        if step < chunks - 1:
            for side in range(2):
                col_copy(step, side).start()
        else:
            other = 1 - lax.rem(me_g, 2)
            col_copy(step, other).start()
            col_recv[me_g] = col_send[step, lax.rem(me_g, 2)]

    lag = 4
    for step in range(chunks):
        produce(step)
        if step >= lag:
            consume(step - lag)
    for step in range(max(chunks - lag, 0), chunks):
        if step == max(chunks - 2, 0):
            attend_at(1)
        if step == chunks - 1:
            attend_at(2)
        consume(step)
    attend_at(3)

    loads[4].wait()
    for r in range(1, group_count):
        source = lax.rem(me_g + r, group_count)
        remote(
            col_send.at[0, 0],
            col_recv.at[source],
            col_send_sem.at[0, 0],
            col_recv_sem.at[source],
            source,
            me_d,
        ).wait_recv()
    for g in range(group_count):
        part = col_recv[g].astype(f32)
        for q in range(4):
            col32[tokens * g : tokens * (g + 1), q * pack_width : q * pack_width + widths[q]] = part[
                tokens * q : tokens * (q + 1), : widths[q]
            ]
    partial = lax.dot_general(
        col32[...].astype(bf16), w_kv[...], (((1,), (1,)), ((), ())), preferred_element_type=f32
    )
    for g in range(group_count):
        part_send[g] = partial[tokens * g : tokens * (g + 1), :]

    def part_copy(r):
        dest = lax.rem(me_g + r, group_count)
        return remote(
            part_send.at[dest],
            part_recv.at[me_g],
            part_send_sem.at[r],
            part_recv_sem.at[me_g],
            dest,
            me_d,
        )

    for r in range(1, group_count):
        part_copy(r).start()
    part_recv[me_g] = part_send[me_g]
    attend_at(4)

    for g in range(group_count):
        part = next_pack[g]
        for q in range(4):
            start = g * block + q * pack_width
            next32[:, start : start + widths[q]] = part[tokens * q : tokens * (q + 1), : widths[q]]
    out_residual[...] = next32[...].astype(bf16)
    squares = jnp.sum(square_acc[...], axis=1, keepdims=True)
    squares = sum(squares[tokens * q : tokens * (q + 1)] for q in range(4))
    row_scale = lax.rsqrt(squares * (1.0 / width) + epsilon)

    for r in range(1, group_count):
        source = lax.rem(me_g + r, group_count)
        remote(
            part_send.at[source],
            part_recv.at[source],
            part_send_sem.at[r],
            part_recv_sem.at[source],
            source,
            me_d,
        ).wait_recv()
    kv_rows = part_recv[0]
    for g in range(1, group_count):
        kv_rows = kv_rows + part_recv[g]
    kv_rows = kv_rows * row_scale
    latent = kv_rows[:, :LAT]
    latent = latent * lax.rsqrt(jnp.mean(latent * latent, axis=1, keepdims=True) + epsilon)
    kv_gain = kv_gain_ref[...].astype(f32)
    latent = jnp.concatenate(
        [latent[:, j * 128 : (j + 1) * 128] * kv_gain[j : j + 1] for j in range(LAT // 128)],
        axis=1,
    ).astype(bf16)
    first_half = kv_rows[:, LAT : LAT + half_width]
    second_half = kv_rows[:, LAT + half_width :]
    cos, sin = rope_cos[...], rope_sin[...]
    rotated = jnp.concatenate(
        [first_half * cos - second_half * sin, second_half * cos + first_half * sin], axis=1
    ).astype(bf16)
    out_entry[:, :LAT] = latent
    out_entry[:, LAT:] = rotated
    latent = latent.astype(f32)
    rotated = rotated.astype(f32)
    for t in range(tokens):
        new_lat = latent[t : t + 1]
        self_score = (
            jnp.sum(q_lat[t].astype(f32) * new_lat, axis=1, keepdims=True)
            + jnp.sum(q_rope[t].astype(f32) * rotated[t : t + 1], axis=1, keepdims=True)
        ) * score_scale
        old = attn_max[t]
        largest = jnp.maximum(old, self_score)
        shrink = jnp.exp(old - largest)
        self_exp = jnp.exp(self_score - largest)
        inverse = 1.0 / (attn_sum[t] * shrink + self_exp)
        self_prob = self_exp.astype(bf16).astype(f32)
        out_attn[t] = (
            attn_acc[t] * (shrink * inverse) + (self_prob * inverse) * new_lat
        ).astype(bf16)

    for r in range(1, dev_count):
        for half in range(2):
            disp_copy(half, r).wait_send()
        for step in range(chunks):
            ret_copy(step, r).wait_send()
    for step in range(chunks - 1):
        for side in range(2):
            col_copy(step, side).wait_send()
    col_copy(chunks - 1, 1 - lax.rem(me_g, 2)).wait_send()
    for r in range(1, group_count):
        part_copy(r).wait_send()


def fused(
    residual,
    routes,
    gate_weights,
    moe_gain,
    attn_gain,
    kv_gain,
    w_gate,
    w_up,
    w_down,
    w_kv,
    q_lat,
    q_rope,
    cache_lat,
    cache_rope,
    page_table,
    lengths,
):
    groups, devs = lax.axis_size("grp"), lax.axis_size("dev")
    tokens, width = residual.shape
    rows = tokens * devs
    units = w_gate.shape[1]
    chunks = groups // 2
    block = width // groups
    pack_width = -(-block // 512) * 128
    k_rows = width // 2 // K_STEPS
    k_chunks = width // k_rows
    w_kv = w_kv.T
    kv_width = w_kv.shape[0]
    f32, bf16 = jnp.float32, jnp.bfloat16
    vmem = pl.BlockSpec(memory_space=pltpu.VMEM)
    smem = pl.BlockSpec(memory_space=pltpu.SMEM)
    hbm = pl.BlockSpec(memory_space=pl.ANY)
    dma = pltpu.SemaphoreType.DMA
    scratch = [
        pltpu.VMEM((k_chunks, k_rows, units), bf16),
        pltpu.VMEM((k_chunks, k_rows, units), bf16),
        pltpu.VMEM((chunks, units, width // chunks), bf16),
        pltpu.VMEM(w_kv.shape, bf16),
        pltpu.VMEM(q_lat.shape, bf16),
        pltpu.VMEM(q_rope.shape, bf16),
        pltpu.VMEM(cache_lat.shape, bf16),
        pltpu.VMEM(cache_rope.shape, bf16),
        pltpu.VMEM((2, 4 * tokens, width // 8), f32),
        pltpu.VMEM((2, 4 * tokens, width // 8), bf16),
        pltpu.VMEM((2, devs, 4 * tokens, width // 8), bf16),
        pltpu.VMEM((rows, width // 2), f32),
        pltpu.VMEM((k_chunks, rows, k_rows), bf16),
        pltpu.VMEM((rows, units), f32),
        pltpu.VMEM((rows, units), f32),
        pltpu.VMEM((rows, units), bf16),
        pltpu.VMEM((devs, 4 * tokens, 128), f32),
        pltpu.VMEM((groups, 4 * tokens, pack_width), f32),
        pltpu.VMEM((groups, 4 * tokens, pack_width), f32),
        pltpu.VMEM((groups, 4 * tokens, pack_width), f32),
        pltpu.VMEM((4 * tokens, pack_width), f32),
        pltpu.VMEM((chunks, devs, 2, 4 * tokens, pack_width), bf16),
        pltpu.VMEM((chunks, devs, 2, 4 * tokens, pack_width), bf16),
        pltpu.VMEM((chunks, 2, 4 * tokens, pack_width), bf16),
        pltpu.VMEM((groups, 4 * tokens, pack_width), bf16),
        pltpu.VMEM((groups * tokens, block), f32),
        pltpu.VMEM((groups, tokens, kv_width), f32),
        pltpu.VMEM((groups, tokens, kv_width), f32),
        pltpu.VMEM((tokens, HEADS, LAT), f32),
        pltpu.VMEM((tokens, HEADS, 1), f32),
        pltpu.VMEM((tokens, HEADS, 1), f32),
        pltpu.VMEM((tokens, ROPE // 2), f32),
        pltpu.VMEM((tokens, ROPE // 2), f32),
        pltpu.VMEM((tokens, width), f32),
        dma((5,)),
        dma((k_chunks,)),
        dma((k_chunks,)),
        dma((chunks,)),
        dma((2, devs)),
        dma((2, devs)),
        dma((chunks, devs)),
        dma((chunks, devs)),
        dma((chunks, 2)),
        dma((groups,)),
        dma((groups,)),
        dma((groups,)),
    ]
    results = pl.pallas_call(
        functools.partial(fused_kernel, groups, devs),
        out_shape=(
            jax.ShapeDtypeStruct(residual.shape, bf16),
            jax.ShapeDtypeStruct((tokens, kv_width), bf16),
            jax.ShapeDtypeStruct(q_lat.shape, bf16),
        ),
        in_specs=[vmem] * 6 + [smem] * 2 + [hbm] * 8,
        out_specs=(vmem, vmem, vmem),
        scratch_shapes=scratch,
        compiler_params=pltpu.CompilerParams(
            collective_id=0, has_side_effects=True, vmem_limit_bytes=58 * 1024 * 1024
        ),
        cost_estimate=pl.CostEstimate(
            flops=1000000000, bytes_accessed=48000000, transcendentals=200000
        ),
    )(
        residual,
        routes.T,
        gate_weights.T,
        moe_gain.reshape(-1, 128),
        attn_gain.reshape(-1, 128),
        kv_gain.reshape(-1, 128),
        lengths,
        page_table,
        w_gate,
        w_up,
        w_down,
        w_kv,
        q_lat,
        q_rope,
        cache_lat,
        cache_rope,
    )
    return pl.pallas_call(
        copy_kernel,
        out_shape=tuple(jax.ShapeDtypeStruct(one.shape, one.dtype) for one in results),
        in_specs=[vmem] * 3,
        out_specs=(vmem,) * 3,
    )(*results)


def copy_kernel(residual_in, entry_in, attn_in, residual_out, entry_out, attn_out):
    residual_out[...] = residual_in[...]
    entry_out[...] = entry_in[...]
    attn_out[...] = attn_in[...]


def fits_fused(mesh):
    groups, devs = mesh.shape["grp"], mesh.shape["dev"]
    return devs == EXPERTS and groups % 2 == 0 and WIDTH % (128 * groups) == 0


def solution(mesh):
    body = fused if fits_fused(mesh) else local
    in_specs = (
        P(("grp", "dev"), None),
        P(("grp", "dev"), None),
        P(("grp", "dev"), None),
        P(),
        P(),
        P(),
        P(None, "dev"),
        P(None, "dev"),
        P("dev", None),
        P("grp", None),
        P(("grp", "dev"), None, None),
        P(("grp", "dev"), None, None),
        P(("grp", "dev"), None, None),
        P(("grp", "dev"), None, None),
        P(("grp", "dev"), None),
        P(("grp", "dev")),
    )
    out_specs = (P(("grp", "dev"), None), P(("grp", "dev"), None), P(("grp", "dev"), None, None))
    return jax.shard_map(body, mesh=mesh, in_specs=in_specs, out_specs=out_specs, check_vma=False)
```
